512 devices in a mesh: lon: 64 (over x, y, z_hi, core), lat: 8 (over z_lo).
Axes of the slice: x: 4, y: 4, z: 16 (z_hi: 2, z_lo: 8; z = z_hi * 8 + z_lo), core: 2. Of those that a mesh axis runs over, the one named last changes fastest.
Arguments:
- sketch: float32 [64, 1024, 2048], P(None, 'lon', 'lat'), may hold values from -6 to 6
- probe_bits: int32 [2, 1024, 2048], P(None, 'lon', 'lat'), may hold values from 0 to 65535
- ocean: int32 [1024, 2048], P('lon', 'lat'), may hold values 0 or 1
- east_cond: float32 [1024, 2048], P('lon', 'lat'), may hold values from 0.2 to 2
- north_cond: float32 [1024, 2048], P('lon', 'lat'), may hold values from 0.1 to 1
- kappa_sq: float32 [1024, 2048], P('lon', 'lat'), may hold values from 0.05 to 0.5
- inv_area: float32 [1024, 2048], P('lon', 'lat'), may hold values from 0.05 to 0.2
Outputs:
- image_out: float32 [64, 1024, 2048], P(None, 'lon', 'lat')
- gram_out: float32 [96, 96], replicated
The draws below stay inside these ranges and needn't reach their ends.
Inputs may be any that keep to these rules, and one draw needn't show every extreme that they name: `probe_bits`: each word holds 16 independent sign bits, bit b of word w giving probe column 16 w + b.
All inputs are finite; a program needn't handle non-finite values. No bound on the sum of `ocean` on one device may be relied on, other than what follows from the above.
Results may differ from the reference program's by a relative error of at most 0.00015.
Values sent between devices are 32-bit elements; how exact they have to be, the bound alone decides.
A program may use at most 64 MiB of HBM per device.

```python
import math
import jax
import jax.numpy as jnp
from jax import lax

SKETCH = 64
WORDS = 2
NLON = 1024
NLAT = 2048


def place_ends(drawn, rng, least, high):
    longest = drawn.shape.index(max(drawn.shape))
    spots = []
    for shift in (0, 1):
        where = [jax.random.randint(jax.random.fold_in(rng, axis), (), 0, length) for axis, length in enumerate(drawn.shape)]
        where[longest] = (where[longest] + shift) % drawn.shape[longest]
        spots.append(tuple(where))
    return drawn.at[spots[0]].set(least).at[spots[1]].set(high)


def steps_of(own_key, extent, split, low, top_value):
    loudness = 1.0
    for position, shards_of in split:
        draws = jax.random.uniform(jax.random.fold_in(jax.random.fold_in(own_key, 6), position), (shards_of,), jnp.float32, low / len(split), top_value / len(split))
        loudness = loudness * jnp.repeat(jnp.exp(draws), extent[position] // shards_of).reshape((-1,) + (1,) * (len(extent) - 1 - position))
    return loudness


def gaussian(stream_key, shape, spread, limit, pieces=(), kind=jnp.bfloat16):
    factor_of = steps_of(stream_key, shape, pieces, -0.22, 0.18) if pieces else 1.0
    result = jax.random.normal(stream_key, shape, jnp.float32) * spread * factor_of
    return jnp.minimum(jnp.maximum(result, -limit), limit).astype(kind)


def setup_inputs(seed: int = 0) -> dict:
    keys = jax.random.split(jax.random.key(seed), 8)
    return {
        "sketch": gaussian(keys[0], (SKETCH, NLON, NLAT), 1.0, 6.0, ((1, 64), (2, 8)), jnp.float32),
        "probe_bits": place_ends(jax.random.randint(keys[1], (WORDS, NLON, NLAT), 0, 65536), jax.random.fold_in(keys[1], 1), 0, 65535).astype(jnp.int32),
        "ocean": place_ends((jax.random.randint(keys[2], (NLON, NLAT), 0, 4) < 3).astype(jnp.int32), jax.random.fold_in(keys[2], 1), 0, 1),
        "east_cond": jnp.clip(jnp.exp(math.log(2.0) - 2.3025851 * jax.random.uniform(keys[3], (NLON, NLAT), jnp.float32) ** steps_of(keys[3], (NLON, NLAT), ((0, 64), (1, 8)), -0.2, 0.2)), 0.2, 2.0),
        "north_cond": jnp.clip(jnp.exp(math.log(1.0) - 2.3025851 * jax.random.uniform(keys[4], (NLON, NLAT), jnp.float32) ** steps_of(keys[4], (NLON, NLAT), ((0, 64), (1, 8)), -0.2, 0.2)), 0.1, 1.0),
        "kappa_sq": jnp.clip(jnp.exp(math.log(0.5) - 2.3025851 * jax.random.uniform(keys[5], (NLON, NLAT), jnp.float32) ** steps_of(keys[5], (NLON, NLAT), ((0, 64), (1, 8)), -0.2, 0.2)), 0.05, 0.5),
        "inv_area": jnp.clip(jnp.exp(math.log(0.2) - 1.3862944 * jax.random.uniform(keys[6], (NLON, NLAT), jnp.float32) ** steps_of(keys[6], (NLON, NLAT), ((0, 64), (1, 8)), -0.2, 0.2)), 0.05, 0.2),
    }


def sign_columns(probe_bits):
    shifts = jnp.arange(16, dtype=jnp.int32)
    picked = jnp.right_shift(probe_bits[:, None], shifts[None, :, None, None])
    flipped = jnp.bitwise_and(picked, 1)
    return (1 - 2 * flipped).astype(jnp.float32).reshape((-1,) + probe_bits.shape[1:])


def reference(sketch, probe_bits, ocean, east_cond, north_cond, kappa_sq, inv_area):
    sea_mask = ocean.astype(jnp.float32)
    column_zero = jnp.zeros((sea_mask.shape[0], 1), jnp.float32)
    east_weight = east_cond * sea_mask * jnp.roll(sea_mask, -1, axis=0)
    north_mask = jnp.concatenate([sea_mask[:, 1:], column_zero], axis=1)
    north_weight = north_cond * sea_mask * north_mask
    west_weight = jnp.roll(east_weight, 1, axis=0)
    south_weight = jnp.concatenate([column_zero, north_weight[:, :-1]], axis=1)
    center_term = kappa_sq + east_weight + west_weight + north_weight + south_weight

    def operate(field_in):
        edge_zero = jnp.zeros(field_in.shape[:2] + (1,), jnp.float32)
        east_val = jnp.roll(field_in, -1, axis=1)
        west_val = jnp.roll(field_in, 1, axis=1)
        north_val = jnp.concatenate([field_in[:, :, 1:], edge_zero], axis=2)
        south_val = jnp.concatenate([edge_zero, field_in[:, :, :-1]], axis=2)
        return sea_mask * (center_term * field_in - east_weight * east_val - west_weight * west_val
                           - north_weight * north_val - south_weight * south_val)

    columns = jnp.concatenate([sketch, sign_columns(probe_bits)], axis=0) * sea_mask
    width_all = columns.shape[0]
    blocks = columns.reshape(width_all // 16, 16, NLON, NLAT)
    flat_all = columns.reshape(width_all, -1)

    def one_block(block):
        second = operate(inv_area * operate(block))
        part_gram = jnp.dot(second.reshape(16, -1), flat_all.T, precision=lax.Precision.HIGHEST)
        return second, part_gram

    seconds, gram_rows = lax.map(one_block, blocks)
    image_out = seconds.reshape(width_all, NLON, NLAT)[:SKETCH]
    gram_out = gram_rows.reshape(width_all, width_all) / (NLON * NLAT)
    return image_out, gram_out
```

```python
import jax
import jax.numpy as jnp
from jax import lax
from jax.experimental import pallas as pl
from jax.experimental.pallas import tpu as pltpu
from jax.sharding import PartitionSpec as P

MESH = pl.DeviceIdType.MESH
SK = 64
NP = 32
NC = SK + NP
I = 16
J = 256
EX = SK
MSG = SK + 8
SG = MSG
ROWS = MSG + NP
PLANE = 32
NZ = 16
PIECE = NC // PLANE
CELLS = 2097152.0


def device_at(x, y, z, c):
    return (((x * 4 + y) * 2 + z // 8) * 2 + c, z % 8)


def lane_iota(rows):
    return lax.broadcasted_iota(jnp.int32, (rows, 128), 1)


def roll(v, shift):
    return pltpu.roll(v, shift, 1)


def shift_north(u, halo):
    left, right = u[:, :128], u[:, 128:]
    rl, rr = roll(left, 127), roll(right, 127)
    last = lane_iota(u.shape[0]) == 127
    return jnp.concatenate([jnp.where(last, rr, rl), jnp.where(last, halo, rr)], axis=1)


def shift_south(u, halo):
    left, right = u[:, :128], u[:, 128:]
    rl, rr = roll(left, 1), roll(right, 1)
    first = lane_iota(u.shape[0]) == 0
    return jnp.concatenate([jnp.where(first, halo, rl), jnp.where(first, rl, rr)], axis=1)


def signs(word, rows):
    bit = lax.broadcasted_iota(jnp.int32, (16, word.shape[1]), 0)
    spread = jnp.broadcast_to(word, (16, word.shape[1]))
    return (1 - 2 * jnp.bitwise_and(jnp.right_shift(spread, bit), 1)).astype(jnp.float32)


def kernel(
    sketch, words, ocean, east, north, kappa, area,
    image, gram,
    s, w_in, oc_in, co_in, cf, haloW, haloE, sgn, packN, packS, recN, recS, edge, edN, edS,
    flux, halo2W, halo2E, out, mats, acc, pieces, rs, zb, ag,
    load_sem, small_sem, lon_send, lon_recv, lat_send, lat_recv, lon2_send, lon2_recv,
    lat2_send, lat2_recv, ar_send, ar_recv, store_sem,
):
    lon, lat = lax.axis_index("lon"), lax.axis_index("lat")
    c, zh = lax.rem(lon, 2), lax.rem(lon // 2, 2)
    y, x = lax.rem(lon // 4, 4), lon // 16
    z = zh * 8 + lat
    rank = (x * 4 + y) * 2 + c
    to_east = (lax.rem(lon + 1, 64), lat)
    to_west = (lax.rem(lon + 63, 64), lat)
    to_north = (lon, lat + 1)
    to_south = (lon, lat - 1)

    plane = []
    for p in range(1, PLANE):
        q = lax.rem(rank + p, PLANE)
        plane.append((q, device_at(q // 8, lax.rem(q // 2, 4), z, lax.rem(q, 2))))
    line = [device_at(x, y, lax.rem(z + p, NZ), c) for p in range(1, NZ)]

    recN[...] = jnp.zeros((2, 16, 128), jnp.float32)
    recS[...] = jnp.zeros((2, 16, 128), jnp.float32)

    barrier = pltpu.get_barrier_semaphore()
    peers = [to_east, to_west] + line + [d for _, d in plane]
    for d in peers:
        pl.semaphore_signal(barrier, inc=1, device_id=d, device_id_type=MESH)

    def load_row(i):
        return pltpu.make_async_copy(sketch.at[:, i, :], s.at[i, pl.ds(0, SK), :], load_sem.at[i])

    small = [
        pltpu.make_async_copy(words, w_in, small_sem.at[0]),
        pltpu.make_async_copy(ocean, oc_in, small_sem.at[1]),
    ] + [
        pltpu.make_async_copy(a, co_in.at[k], small_sem.at[2 + k])
        for k, a in enumerate((east, north, kappa, area))
    ]
    order = [0, I - 1] + list(range(1, I - 1))
    for i in order[:2]:
        load_row(i).start()
    for cp in small:
        cp.start()
    for i in order[2:]:
        load_row(i).start()

    for cp in small:
        cp.wait()

    sea = oc_in[...].astype(jnp.float32)
    for i in (0, I - 1):
        for w in range(2):
            s[i, pl.ds(EX + w, 1), :] = w_in[w, i : i + 1, :].astype(jnp.float32)
        s[i, pl.ds(EX + 2, 1), :] = sea[i : i + 1]
        s[i, pl.ds(EX + 3, 1), :] = co_in[0, i : i + 1, :]
        s[i, pl.ds(EX + 4, 4), :] = jnp.zeros((4, J), jnp.float32)
    for i in order[:2]:
        load_row(i).wait()

    pl.semaphore_wait(barrier, len(peers))

    def remote(src, dst, ss, rsem, d):
        return pltpu.make_async_remote_copy(
            src_ref=src, dst_ref=dst, send_sem=ss, recv_sem=rsem, device_id=d, device_id_type=MESH
        )

    east1 = remote(s.at[I - 1, pl.ds(0, MSG), :], haloW, lon_send.at[0], lon_recv.at[0], to_east)
    west1 = remote(s.at[0, pl.ds(0, MSG), :], haloE, lon_send.at[1], lon_recv.at[1], to_west)
    east1.start()
    west1.start()

    def both_lats(turn):
        ss, rsem = ((lat_send, lat_recv), (lat2_send, lat2_recv))[turn]
        up = remote(packN, recS.at[turn], ss.at[0], rsem.at[0], to_north)
        down = remote(packS, recN.at[turn], ss.at[1], rsem.at[1], to_south)
        return up, down

    def start_lats(turn):
        up, down = both_lats(turn)
        pl.when(lat < 7)(up.start)
        pl.when(lat > 0)(down.start)

    def wait_lats(turn):
        up, down = both_lats(turn)

        @pl.when(lat < 7)
        def _():
            up.wait_send()
            down.wait_recv()

        @pl.when(lat > 0)
        def _():
            down.wait_send()
            up.wait_recv()

    def pack_edges(rows_of):
        edge[...] = jnp.zeros((2, SK, 128), jnp.float32)

        def step(i, carry):
            mine = lane_iota(8) == i
            for g in range(SK // 8):
                rows = pl.ds(8 * g, 8)
                v = rows_of(i, rows)
                edge[0, rows, :] = jnp.where(mine, roll(v[:, 128:], i + 1), edge[0, rows, :])
                edge[1, rows, :] = jnp.where(mine, roll(v[:, :128], i), edge[1, rows, :])
            return carry

        lax.fori_loop(0, I, step, 0)
        for side, pack in enumerate((packN, packS)):
            total = edge[side, 0:8, :]
            for g in range(1, SK // 8):
                total = total + roll(edge[side, 8 * g : 8 * g + 8, :], 16 * g)
            pack[0:8, :] = total

    for i in order[2:]:
        load_row(i).wait()

    w0f, w1f = w_in[0].astype(jnp.float32), w_in[1].astype(jnp.float32)
    north_c = co_in[1]
    sides = [a[:, h * 128 : h * 128 + 128] for h in (1, 0) for a in (w0f, w1f, sea, north_c)]
    turned = jnp.transpose(jnp.concatenate(sides, axis=0))
    packN[8:16, :] = jnp.broadcast_to(turned[127:128, :], (8, 128))
    packS[8:16, :] = jnp.broadcast_to(roll(turned[0:1, :], 64), (8, 128))
    pack_edges(lambda i, rows: s[i, rows, :])
    start_lats(0)

    def own_signs(i, carry):
        for w in range(2):
            s[i, pl.ds(SG + 16 * w, 16), :] = signs(w_in[w, pl.ds(i, 1), :], 16)
        return carry

    lax.fori_loop(0, I, own_signs, 0)
    mats[...] = jnp.zeros(mats.shape, jnp.bfloat16)
    acc[...] = jnp.zeros(acc.shape, jnp.float32)

    wait_lats(0)

    def column_of(rec):
        square = jnp.transpose(jnp.broadcast_to(rec[0, 8:9, :], (128, 128)))
        return square[32:48, :], square[48:64, :]

    sea_n, _ = column_of(recN)
    sea_s, north_s = column_of(recS)
    w_n = north_c * sea * shift_north(sea, sea_n)
    w_s = shift_south(w_n, north_s * sea_s * sea[:, :128])
    cf[3] = w_n
    cf[4] = w_s
    cf[5] = co_in[3]
    cf[6] = jnp.sqrt(co_in[3])
    inner_e = co_in[0, 0 : I - 1, :] * sea[0 : I - 1] * sea[1:I]
    cf[1, 0 : I - 1, :] = inner_e
    cf[2, 1:I, :] = inner_e
    kap = co_in[2]
    mid = slice(1, I - 1)
    cf[0, mid, :] = sea[mid] * (
        kap[mid] + cf[1, mid, :] + cf[2, mid, :] + w_n[mid] + w_s[mid]
    )

    def spread(turn, rec, ed):
        for g in range(SK // 8):
            v = rec[turn, 0:8, :]
            ed[8 * g : 8 * g + 8, :] = v if g == 0 else roll(v, 128 - 16 * g)

    def spread_signs(rec, ed):
        ints = rec[0, 8:9, :].astype(jnp.int32)
        for w in range(2):
            v = signs(ints, 16)
            ed[SK + 16 * w : SK + 16 * w + 16, :] = v if w == 0 else roll(v, 128 - 16)

    for rec, ed in ((recN, edN), (recS, edS)):
        spread(0, rec, ed)
        spread_signs(rec, ed)

    def weights(i):
        return [cf[k, pl.ds(i, 1), :] for k in range(7)]

    def stencil(i, wt, here, there_e, there_w, erows):
        hn = roll(edN[erows, :], 127 - i)
        hs = roll(edS[erows, :], lax.rem(128 - i, 128))
        return (
            wt[0] * here
            - wt[1] * there_e
            - wt[2] * there_w
            - wt[3] * shift_north(here, hn)
            - wt[4] * shift_south(here, hs)
        )

    def first_row(i, east_of, west_of):
        wt = weights(i)
        for g in range(NC // 16):
            at = 16 * g if g < SK // 16 else SG + 16 * g - SK
            rows = pl.ds(at, 16)
            f = stencil(
                i, wt, s[i, rows, :], east_of(g, rows), west_of(g, rows), pl.ds(16 * g, 16)
            )
            if g < SK // 16:
                flux[i, rows, :] = wt[5] * f
            t = wt[6] * f
            high = t.astype(jnp.bfloat16)
            mats[i, pl.ds(16 * g, 16), :] = high
            mats[i, pl.ds(128 + 16 * g, 16), :] = (t - high.astype(jnp.float32)).astype(
                jnp.bfloat16
            )
        m = mats[i]
        acc[...] += lax.dot_general(
            m, m, (((1,), (1,)), ((), ())), preferred_element_type=jnp.float32
        )

    def inner_first(i, carry):
        first_row(i, lambda g, rows: s[i + 1, rows, :], lambda g, rows: s[i - 1, rows, :])
        return carry

    lax.fori_loop(1, I - 1, inner_first, 0)

    east1.wait()
    west1.wait()
    sea_e, sea_w = haloE[EX + 2 : EX + 3, :], haloW[EX + 2 : EX + 3, :]
    cf[1, I - 1 : I, :] = co_in[0, I - 1 : I, :] * sea[I - 1 : I] * sea_e
    cf[2, 0:1, :] = haloW[EX + 3 : EX + 4, :] * sea_w * sea[0:1]
    for i in (0, I - 1):
        r = slice(i, i + 1)
        cf[0, r, :] = sea[r] * (kap[r] + cf[1, r, :] + cf[2, r, :] + w_n[r] + w_s[r])
    for side, halo in enumerate((haloW, haloE)):
        for w in range(2):
            sgn[side, 16 * w : 16 * w + 16, :] = signs(
                halo[EX + w : EX + w + 1, :].astype(jnp.int32), 16
            )

    def halo_of(side, halo):
        def at(g, rows):
            if g < SK // 16:
                return halo[rows, :]
            return sgn[side, 16 * g - SK : 16 * g - SK + 16, :]

        return at

    first_row(0, lambda g, rows: s[1, rows, :], halo_of(0, haloW))
    first_row(I - 1, halo_of(1, haloE), lambda g, rows: s[I - 2, rows, :])

    east2 = remote(flux.at[I - 1], halo2W, lon2_send.at[0], lon2_recv.at[0], to_east)
    west2 = remote(flux.at[0], halo2E, lon2_send.at[1], lon2_recv.at[1], to_west)

    total = (acc[0:NC, 0:128] + acc[0:NC, 128:256]) + (
        acc[128 : 128 + NC, 0:128] + acc[128 : 128 + NC, 128:256]
    )
    for q in range(PLANE):
        pieces[q] = total[PIECE * q : PIECE * q + PIECE, :]
    for q, d in plane:
        remote(pieces.at[q], rs.at[rank], ar_send.at[0], ar_recv.at[0], d).start()
    east2.start()
    west2.start()
    rs[rank] = pieces[rank]

    pack_edges(lambda i, rows: flux[i, rows, :])
    start_lats(1)

    def wait_all(ref, n, sem):
        pltpu.make_async_copy(ref.at[pl.ds(0, n)], ref.at[pl.ds(0, n)], sem).wait()

    wait_all(rs, PLANE - 1, ar_recv.at[0])
    zb[z] = jnp.sum(rs[...], axis=0)
    for d in line:
        remote(zb.at[z], zb.at[z], ar_send.at[1], ar_recv.at[1], d).start()
    wait_all(rs, PLANE - 1, ar_send.at[0])

    wait_lats(1)
    for rec, ed in ((recN, edN), (recS, edS)):
        spread(1, rec, ed)

    def second_row(i, east_of, west_of):
        wt = weights(i)
        for g in range(SK // 16):
            rows = pl.ds(16 * g, 16)
            out[i, rows, :] = stencil(i, wt, flux[i, rows, :], east_of(rows), west_of(rows), rows)

    def inner_second(i, carry):
        second_row(i, lambda rows: flux[i + 1, rows, :], lambda rows: flux[i - 1, rows, :])
        return carry

    lax.fori_loop(1, I - 1, inner_second, 0)

    def store_row(i):
        return pltpu.make_async_copy(out.at[i], image.at[:, i, :], store_sem.at[i])

    for i in range(1, I - 1):
        store_row(i).start()

    wait_all(zb, NZ - 1, ar_recv.at[1])
    wait_all(zb, NZ - 1, ar_send.at[1])
    ag[rank] = jnp.sum(zb[...], axis=0) * (1.0 / CELLS)
    for _, d in plane:
        remote(ag.at[rank], ag.at[rank], ar_send.at[2], ar_recv.at[2], d).start()

    east2.wait()
    west2.wait()
    second_row(0, lambda rows: flux[1, rows, :], lambda rows: halo2W[rows, :])
    second_row(I - 1, lambda rows: halo2E[rows, :], lambda rows: flux[I - 2, rows, :])
    for i in (0, I - 1):
        store_row(i).start()
    wait_all(ag, PLANE - 1, ar_recv.at[2])
    wait_all(ag, PLANE - 1, ar_send.at[2])
    gram[...] = ag[...]
    for i in order:
        store_row(i).wait()


def local(sketch, probe_bits, ocean, east_cond, north_cond, kappa_sq, inv_area):
    f32 = jnp.float32

    def vmem(*shape, kind=f32):
        return pltpu.VMEM(shape, kind)

    dma = pltpu.SemaphoreType.DMA
    any_space = pl.BlockSpec(memory_space=pl.ANY)
    image, gram = pl.pallas_call(
        kernel,
        out_shape=(
            jax.ShapeDtypeStruct((SK, I, J), f32),
            jax.ShapeDtypeStruct((PLANE, PIECE, 128), f32),
        ),
        in_specs=[any_space] * 7,
        out_specs=(any_space, pl.BlockSpec(memory_space=pltpu.VMEM)),
        scratch_shapes=[
            vmem(I, ROWS, J),
            vmem(2, I, J, kind=jnp.int32),
            vmem(I, J, kind=jnp.int32),
            vmem(4, I, J),
            vmem(7, I, J),
            vmem(MSG, J),
            vmem(MSG, J),
            vmem(2, NP, J),
            vmem(16, 128),
            vmem(16, 128),
            vmem(2, 16, 128),
            vmem(2, 16, 128),
            vmem(2, SK, 128),
            vmem(NC, 128),
            vmem(NC, 128),
            vmem(I, SK, J),
            vmem(SK, J),
            vmem(SK, J),
            vmem(I, SK, J),
            vmem(I, 256, J, kind=jnp.bfloat16),
            vmem(256, 256),
            vmem(PLANE, PIECE, 128),
            vmem(PLANE, PIECE, 128),
            vmem(NZ, PIECE, 128),
            vmem(PLANE, PIECE, 128),
            dma((I,)),
            dma((6,)),
            dma((2,)),
            dma((2,)),
            dma((2,)),
            dma((2,)),
            dma((2,)),
            dma((2,)),
            dma((2,)),
            dma((2,)),
            dma((3,)),
            dma((3,)),
            dma((I,)),
        ],
        compiler_params=pltpu.CompilerParams(
            collective_id=0, has_side_effects=True, vmem_limit_bytes=56 * 2**20
        ),
        name="nystrom",
    )(sketch, probe_bits, ocean, east_cond, north_cond, kappa_sq, inv_area)
    return image, gram.reshape(NC, 128)[:, :NC]


def solution(mesh):
    cells = P("lon", "lat")
    columns = P(None, "lon", "lat")
    return jax.shard_map(
        local,
        mesh=mesh,
        in_specs=(columns, columns, cells, cells, cells, cells, cells),
        out_specs=(columns, P()),
        check_vma=False,
    )
```

```python
import jax
import jax.numpy as jnp
from jax import lax
from jax.experimental import pallas as pl
from jax.experimental.pallas import tpu as pltpu
from jax.sharding import PartitionSpec as P

MESH = pl.DeviceIdType.MESH
SK = 64
NP = 32
NC = SK + NP
I = 16
J = 256
EX = SK
MSG = SK + 8
SG = MSG
ROWS = MSG + NP
PLANE = 32
NZ = 16
PIECE = NC // PLANE
CELLS = 2097152.0
CHUNKS = ((0, 40), (40, MSG - 40))
STEPS = sorted(
    ((dx, dy, dc) for dx in range(4) for dy in range(4) for dc in range(2) if dx or dy or dc),
    key=lambda d: (-min(d[0], 4 - d[0]) - min(d[1], 4 - d[1]), -d[2]),
)
LINE = sorted(range(1, NZ), key=lambda d: -min(d, NZ - d))


def device_at(x, y, z, c):
    return (((x * 4 + y) * 2 + z // 8) * 2 + c, z % 8)


def lane_iota(rows):
    return lax.broadcasted_iota(jnp.int32, (rows, 128), 1)


def roll(v, shift):
    return pltpu.roll(v, shift, 1)


def shift_north(u, halo):
    left, right = u[:, :128], u[:, 128:]
    rl, rr = roll(left, 127), roll(right, 127)
    last = lane_iota(u.shape[0]) == 127
    return jnp.concatenate([jnp.where(last, rr, rl), jnp.where(last, halo, rr)], axis=1)


def shift_south(u, halo):
    left, right = u[:, :128], u[:, 128:]
    rl, rr = roll(left, 1), roll(right, 1)
    first = lane_iota(u.shape[0]) == 0
    return jnp.concatenate([jnp.where(first, halo, rl), jnp.where(first, rl, rr)], axis=1)


def signs(word, rows):
    bit = lax.broadcasted_iota(jnp.int32, (16, word.shape[1]), 0)
    spread = jnp.broadcast_to(word, (16, word.shape[1]))
    return (1 - 2 * jnp.bitwise_and(jnp.right_shift(spread, bit), 1)).astype(jnp.float32)


def kernel(
    sketch, words, ocean, east, north, kappa, area,
    image, gram,
    s, w_in, oc_in, co_in, cf, halo, via, sgn, packN, packS, recN, recS, edge, edN, edS,
    flux, halo2W, halo2E, out, mats, acc, pieces, rs, zb, ag,
    load_sem, small_sem, far_send, via_recv, fwd_send, far_recv, near_send, near_recv, rounds, lat_send, lat_recv, lon2_send, lon2_recv,
    lat2_send, lat2_recv, ar_send, ar_recv, store_sem,
):
    lon, lat = lax.axis_index("lon"), lax.axis_index("lat")
    c, zh = lax.rem(lon, 2), lax.rem(lon // 2, 2)
    y, x = lax.rem(lon // 4, 4), lon // 16
    z = zh * 8 + lat
    rank = (x * 4 + y) * 2 + c
    to_east = (lax.rem(lon + 1, 64), lat)
    to_west = (lax.rem(lon + 63, 64), lat)
    to_north = (lon, lat + 1)
    to_south = (lon, lat - 1)

    far_lon, near_lon = lax.rem(lon + 63 + 2 * c, 64), lon + 1 - 2 * c
    lat4 = lax.rem(lat + 4, 8)
    far_row, near_row = c * (I - 1), (1 - c) * (I - 1)

    def at_plane(dx, dy, dc):
        px, py, pc = lax.rem(x + dx, 4), lax.rem(y + dy, 4), lax.rem(c + dc, 2)
        return (px * 4 + py) * 2 + pc, device_at(px, py, z, pc)

    def at_line(d):
        return device_at(x, y, lax.rem(z + d, NZ), c)

    plane = [at_plane(*d) for d in STEPS]
    line = [at_line(d) for d in LINE]

    recN[...] = jnp.zeros((2, 16, 128), jnp.float32)
    recS[...] = jnp.zeros((2, 16, 128), jnp.float32)

    peers = [(far_lon, lat4)]
    peers += [at_line(d) for d in (4, NZ - 4)]
    peers += [at_plane(*d)[1] for d in ((2, 0, 0), (0, 2, 0))]
    peers += [at_line(d) for d in (1, NZ - 1)]
    peers += [at_plane(*d)[1] for d in ((1, 0, 0), (3, 0, 0), (0, 1, 0), (0, 3, 0), (0, 0, 1))]

    def tell(sem):
        for d in peers:
            pl.semaphore_signal(sem, inc=1, device_id=d, device_id_type=MESH)

    barrier = pltpu.get_barrier_semaphore()
    tell(barrier)

    def load_row(i):
        return pltpu.make_async_copy(sketch.at[:, i, :], s.at[i, pl.ds(0, SK), :], load_sem.at[i])

    small = [
        pltpu.make_async_copy(words, w_in, small_sem.at[0]),
        pltpu.make_async_copy(ocean, oc_in, small_sem.at[1]),
    ] + [
        pltpu.make_async_copy(a, co_in.at[k], small_sem.at[2 + k])
        for k, a in enumerate((east, north, kappa, area))
    ]
    order = [0, I - 1] + list(range(1, I - 1))
    for i in order[:2]:
        load_row(i).start()
    for cp in small:
        cp.start()
    for i in order[2:]:
        load_row(i).start()

    for cp in small:
        cp.wait()

    sea = oc_in[...].astype(jnp.float32)
    for i in (0, I - 1):
        for w in range(2):
            s[i, pl.ds(EX + w, 1), :] = w_in[w, i : i + 1, :].astype(jnp.float32)
        s[i, pl.ds(EX + 2, 1), :] = sea[i : i + 1]
        s[i, pl.ds(EX + 3, 1), :] = co_in[0, i : i + 1, :]
        s[i, pl.ds(EX + 4, 4), :] = jnp.zeros((4, J), jnp.float32)
    for i in order[:2]:
        load_row(i).wait()

    def remote(src, dst, ss, rsem, d):
        return pltpu.make_async_remote_copy(
            src_ref=src, dst_ref=dst, send_sem=ss, recv_sem=rsem, device_id=d, device_id_type=MESH
        )

    def both_lats(turn):
        ss, rsem = ((lat_send, lat_recv), (lat2_send, lat2_recv))[turn]
        up = remote(packN, recS.at[turn], ss.at[0], rsem.at[0], to_north)
        down = remote(packS, recN.at[turn], ss.at[1], rsem.at[1], to_south)
        return up, down

    def start_lats(turn):
        up, down = both_lats(turn)
        pl.when(lat < 7)(up.start)
        pl.when(lat > 0)(down.start)

    def wait_lats(turn):
        up, down = both_lats(turn)

        @pl.when(lat < 7)
        def _():
            up.wait_send()
            down.wait_recv()

        @pl.when(lat > 0)
        def _():
            down.wait_send()
            up.wait_recv()

    def pack_edges(rows_of):
        edge[...] = jnp.zeros((2, SK, 128), jnp.float32)

        def step(i, carry):
            mine = lane_iota(8) == i
            for g in range(SK // 8):
                rows = pl.ds(8 * g, 8)
                v = rows_of(i, rows)
                edge[0, rows, :] = jnp.where(mine, roll(v[:, 128:], i + 1), edge[0, rows, :])
                edge[1, rows, :] = jnp.where(mine, roll(v[:, :128], i), edge[1, rows, :])
            return carry

        lax.fori_loop(0, I, step, 0)
        for side, pack in enumerate((packN, packS)):
            total = edge[side, 0:8, :]
            for g in range(1, SK // 8):
                total = total + roll(edge[side, 8 * g : 8 * g + 8, :], 16 * g)
            pack[0:8, :] = total

    for i in order[2:]:
        load_row(i).wait()

    w0f, w1f = w_in[0].astype(jnp.float32), w_in[1].astype(jnp.float32)
    north_c = co_in[1]
    sides = [a[:, h * 128 : h * 128 + 128] for h in (1, 0) for a in (w0f, w1f, sea, north_c)]
    turned = jnp.transpose(jnp.concatenate(sides, axis=0))
    packN[8:16, :] = jnp.broadcast_to(turned[127:128, :], (8, 128))
    packS[8:16, :] = jnp.broadcast_to(roll(turned[0:1, :], 64), (8, 128))
    pack_edges(lambda i, rows: s[i, rows, :])
    def own_signs(i, carry):
        for w in range(2):
            s[i, pl.ds(SG + 16 * w, 16), :] = signs(w_in[w, pl.ds(i, 1), :], 16)
        return carry

    lax.fori_loop(0, I, own_signs, 0)
    mats[...] = jnp.zeros(mats.shape, jnp.bfloat16)
    acc[...] = jnp.zeros(acc.shape, jnp.float32)

    pl.semaphore_wait(barrier, len(peers))

    early = zh == 0

    def part(ref, k):
        return ref.at[pl.ds(*CHUNKS[k]), :]

    def far_copy(via_slot, k, d):
        return remote(
            part(s.at[far_row], k), part(via.at[via_slot], k), far_send.at[k],
            via_recv.at[via_slot, k], d,
        )

    def swap(k):
        return far_copy(0, k, (lon, lat4))

    def lift(k):
        return far_copy(1, k, (far_lon, lat4))

    def forward(via_slot, k):
        slot, d = ((1 - c, (far_lon, lat4)), (c, (lon, lat4)))[via_slot]
        return remote(
            part(via.at[via_slot], k), part(halo.at[slot], k), fwd_send.at[via_slot, k],
            far_recv.at[k], d,
        )

    near = remote(
        s.at[near_row, pl.ds(0, MSG), :], halo.at[c], near_send, near_recv, (near_lon, lat)
    )
    near_in = remote(
        s.at[near_row, pl.ds(0, MSG), :], halo.at[1 - c], near_send, near_recv, (near_lon, lat)
    )

    @pl.when(early)
    def _():
        for k in range(len(CHUNKS)):
            swap(k).start()

    @pl.when(zh == 1)
    def _():
        for k in range(len(CHUNKS)):
            lift(k).start()

    start_lats(0)
    near.start()
    tell(rounds.at[0])

    wait_lats(0)

    def column_of(rec):
        square = jnp.transpose(jnp.broadcast_to(rec[0, 8:9, :], (128, 128)))
        return square[32:48, :], square[48:64, :]

    sea_n, _ = column_of(recN)
    sea_s, north_s = column_of(recS)
    w_n = north_c * sea * shift_north(sea, sea_n)
    w_s = shift_south(w_n, north_s * sea_s * sea[:, :128])
    cf[3] = w_n
    cf[4] = w_s
    cf[5] = co_in[3]
    cf[6] = jnp.sqrt(co_in[3])
    inner_e = co_in[0, 0 : I - 1, :] * sea[0 : I - 1] * sea[1:I]
    cf[1, 0 : I - 1, :] = inner_e
    cf[2, 1:I, :] = inner_e
    kap = co_in[2]
    mid = slice(1, I - 1)
    cf[0, mid, :] = sea[mid] * (
        kap[mid] + cf[1, mid, :] + cf[2, mid, :] + w_n[mid] + w_s[mid]
    )

    def spread(turn, rec, ed):
        for g in range(SK // 8):
            v = rec[turn, 0:8, :]
            ed[8 * g : 8 * g + 8, :] = v if g == 0 else roll(v, 128 - 16 * g)

    def spread_signs(rec, ed):
        ints = rec[0, 8:9, :].astype(jnp.int32)
        for w in range(2):
            v = signs(ints, 16)
            ed[SK + 16 * w : SK + 16 * w + 16, :] = v if w == 0 else roll(v, 128 - 16)

    for rec, ed in ((recN, edN), (recS, edS)):
        spread(0, rec, ed)
        spread_signs(rec, ed)

    def weights(i):
        return [cf[k, pl.ds(i, 1), :] for k in range(7)]

    def stencil(i, wt, here, there_e, there_w, erows):
        hn = roll(edN[erows, :], 127 - i)
        hs = roll(edS[erows, :], lax.rem(128 - i, 128))
        return (
            wt[0] * here
            - wt[1] * there_e
            - wt[2] * there_w
            - wt[3] * shift_north(here, hn)
            - wt[4] * shift_south(here, hs)
        )

    def first_row(i, east_of, west_of):
        wt = weights(i)
        for g in range(NC // 16):
            at = 16 * g if g < SK // 16 else SG + 16 * g - SK
            rows = pl.ds(at, 16)
            f = stencil(
                i, wt, s[i, rows, :], east_of(g, rows), west_of(g, rows), pl.ds(16 * g, 16)
            )
            if g < SK // 16:
                flux[i, rows, :] = wt[5] * f
            t = wt[6] * f
            high = t.astype(jnp.bfloat16)
            mats[i, pl.ds(16 * g, 16), :] = high
            mats[i, pl.ds(128 + 16 * g, 16), :] = (t - high.astype(jnp.float32)).astype(
                jnp.bfloat16
            )
        m = mats[i]
        acc[...] += lax.dot_general(
            m, m, (((1,), (1,)), ((), ())), preferred_element_type=jnp.float32
        )

    def inner_first(i, carry):
        first_row(i, lambda g, rows: s[i + 1, rows, :], lambda g, rows: s[i - 1, rows, :])
        return carry

    @pl.when(early)
    def _():
        for k in range(len(CHUNKS)):
            for via_slot, copy in ((1, lift(k)), (0, swap(k))):
                copy.wait_recv()
                forward(via_slot, k).start()

    pl.semaphore_wait(rounds.at[0], len(peers))
    tell(rounds.at[1])

    lax.fori_loop(1, I - 1, inner_first, 0)

    near_in.wait_recv()
    for k in range(len(CHUNKS)):
        remote(part(halo.at[c], k), part(halo.at[c], k), fwd_send.at[0, k], far_recv.at[k], (lon, lat4)).wait_recv()
    haloW, haloE = halo.at[0], halo.at[1]
    sea_e, sea_w = haloE[EX + 2 : EX + 3, :], haloW[EX + 2 : EX + 3, :]
    cf[1, I - 1 : I, :] = co_in[0, I - 1 : I, :] * sea[I - 1 : I] * sea_e
    cf[2, 0:1, :] = haloW[EX + 3 : EX + 4, :] * sea_w * sea[0:1]
    for i in (0, I - 1):
        r = slice(i, i + 1)
        cf[0, r, :] = sea[r] * (kap[r] + cf[1, r, :] + cf[2, r, :] + w_n[r] + w_s[r])
    for side in range(2):
        for w in range(2):
            sgn[side, 16 * w : 16 * w + 16, :] = signs(
                halo[side, EX + w : EX + w + 1, :].astype(jnp.int32), 16
            )

    def halo_of(side):
        def at(g, rows):
            if g < SK // 16:
                return halo[side, rows, :]
            return sgn[side, 16 * g - SK : 16 * g - SK + 16, :]

        return at

    first_row(0, lambda g, rows: s[1, rows, :], halo_of(0))
    first_row(I - 1, halo_of(1), lambda g, rows: s[I - 2, rows, :])

    east2 = remote(flux.at[I - 1], halo2W, lon2_send.at[0], lon2_recv.at[0], to_east)
    west2 = remote(flux.at[0], halo2E, lon2_send.at[1], lon2_recv.at[1], to_west)

    total = (acc[0:NC, 0:128] + acc[0:NC, 128:256]) + (
        acc[128 : 128 + NC, 0:128] + acc[128 : 128 + NC, 128:256]
    )
    for q in range(PLANE):
        pieces[q] = total[PIECE * q : PIECE * q + PIECE, :]
    pl.semaphore_wait(rounds.at[1], len(peers))
    for q, d in plane:
        remote(pieces.at[q], rs.at[rank], ar_send.at[0], ar_recv.at[0], d).start()
    rs[rank] = pieces[rank]

    pack_edges(lambda i, rows: flux[i, rows, :])
    start_lats(1)

    def wait_all(ref, n, sem):
        pltpu.make_async_copy(ref.at[pl.ds(0, n)], ref.at[pl.ds(0, n)], sem).wait()

    wait_all(rs, PLANE - 1, ar_recv.at[0])
    zb[z] = jnp.sum(rs[...], axis=0)
    for d in line:
        remote(zb.at[z], zb.at[z], ar_send.at[1], ar_recv.at[1], d).start()
    wait_all(rs, PLANE - 1, ar_send.at[0])
    east2.start()
    west2.start()

    wait_lats(1)
    for rec, ed in ((recN, edN), (recS, edS)):
        spread(1, rec, ed)

    def second_row(i, east_of, west_of):
        wt = weights(i)
        for g in range(SK // 16):
            rows = pl.ds(16 * g, 16)
            out[i, rows, :] = stencil(i, wt, flux[i, rows, :], east_of(rows), west_of(rows), rows)

    def inner_second(i, carry):
        second_row(i, lambda rows: flux[i + 1, rows, :], lambda rows: flux[i - 1, rows, :])
        return carry

    lax.fori_loop(1, I - 1, inner_second, 0)

    def store_row(i):
        return pltpu.make_async_copy(out.at[i], image.at[:, i, :], store_sem.at[i])

    for i in range(1, I - 1):
        store_row(i).start()

    wait_all(zb, NZ - 1, ar_recv.at[1])
    wait_all(zb, NZ - 1, ar_send.at[1])
    ag[rank] = jnp.sum(zb[...], axis=0) * (1.0 / CELLS)
    for _, d in plane:
        remote(ag.at[rank], ag.at[rank], ar_send.at[2], ar_recv.at[2], d).start()

    east2.wait()
    west2.wait()
    second_row(0, lambda rows: flux[1, rows, :], lambda rows: halo2W[rows, :])
    second_row(I - 1, lambda rows: halo2E[rows, :], lambda rows: flux[I - 2, rows, :])
    for i in (0, I - 1):
        store_row(i).start()
    wait_all(ag, PLANE - 1, ar_recv.at[2])
    wait_all(ag, PLANE - 1, ar_send.at[2])
    for q in range(PLANE):
        gram[PIECE * q : PIECE * q + PIECE, :] = ag[q, :, 0:NC]
    for i in order:
        store_row(i).wait()
    near.wait_send()
    for k in range(len(CHUNKS)):
        swap(k).wait_send()

    @pl.when(early)
    def _():
        for k in range(len(CHUNKS)):
            for via_slot in range(2):
                forward(via_slot, k).wait_send()


def local(sketch, probe_bits, ocean, east_cond, north_cond, kappa_sq, inv_area):
    f32 = jnp.float32

    def vmem(*shape, kind=f32):
        return pltpu.VMEM(shape, kind)

    dma = pltpu.SemaphoreType.DMA
    any_space = pl.BlockSpec(memory_space=pl.ANY)
    image, gram = pl.pallas_call(
        kernel,
        out_shape=(
            pltpu.VMEM((SK, I, J), f32),
            pltpu.VMEM((NC, NC), f32),
        ),
        in_specs=[pl.BlockSpec(memory_space=pltpu.HBM)] * 7,
        out_specs=(any_space, pl.BlockSpec(memory_space=pltpu.VMEM)),
        scratch_shapes=[
            vmem(I, ROWS, J),
            vmem(2, I, J, kind=jnp.int32),
            vmem(I, J, kind=jnp.int32),
            vmem(4, I, J),
            vmem(7, I, J),
            vmem(2, MSG, J),
            vmem(2, MSG, J),
            vmem(2, NP, J),
            vmem(16, 128),
            vmem(16, 128),
            vmem(2, 16, 128),
            vmem(2, 16, 128),
            vmem(2, SK, 128),
            vmem(NC, 128),
            vmem(NC, 128),
            vmem(I, SK, J),
            vmem(SK, J),
            vmem(SK, J),
            vmem(I, SK, J),
            vmem(I, 256, J, kind=jnp.bfloat16),
            vmem(256, 256),
            vmem(PLANE, PIECE, 128),
            vmem(PLANE, PIECE, 128),
            vmem(NZ, PIECE, 128),
            vmem(PLANE, PIECE, 128),
            dma((I,)),
            dma((6,)),
            dma((len(CHUNKS),)),
            dma((2, len(CHUNKS))),
            dma((2, len(CHUNKS))),
            dma((len(CHUNKS),)),
            dma,
            dma,
            pltpu.SemaphoreType.REGULAR((2,)),
            dma((2,)),
            dma((2,)),
            dma((2,)),
            dma((2,)),
            dma((2,)),
            dma((2,)),
            dma((3,)),
            dma((3,)),
            dma((I,)),
        ],
        compiler_params=pltpu.CompilerParams(
            collective_id=0, has_side_effects=True, vmem_limit_bytes=24 * 2**20
        ),
        name="nystrom",
    )(*[pltpu.with_memory_space_constraint(a, pltpu.HBM) for a in (sketch, probe_bits, ocean, east_cond, north_cond, kappa_sq, inv_area)])
    return image, gram


def solution(mesh):
    cells = P("lon", "lat")
    columns = P(None, "lon", "lat")
    return jax.shard_map(
        local,
        mesh=mesh,
        in_specs=(columns, columns, cells, cells, cells, cells, cells),
        out_specs=(columns, P()),
        check_vma=False,
    )
```

```python
import jax
import jax.numpy as jnp
from jax import lax
from jax.experimental import pallas as pl
from jax.experimental.pallas import tpu as pltpu
from jax.sharding import PartitionSpec as P

MESH = pl.DeviceIdType.MESH
SK = 64
NP = 32
NC = SK + NP
I = 16
J = 256
EX = SK
MSG = SK + 8
SG = MSG
ROWS = MSG + NP
PLANE = 32
NZ = 16
PIECE = NC // PLANE
CELLS = 2097152.0
PK = NC + SK
PKG = PK + 8
RET = SK + 8
STEPS = sorted(
    ((dx, dy, dc) for dx in range(4) for dy in range(4) for dc in range(2) if dx or dy or dc),
    key=lambda d: (-min(d[0], 4 - d[0]) - min(d[1], 4 - d[1]), -d[2]),
)
LINE = sorted(range(1, NZ), key=lambda d: -min(d, NZ - d))


def device_at(x, y, z, c):
    return (((x * 4 + y) * 2 + z // 8) * 2 + c, z % 8)


def lane_iota(rows):
    return lax.broadcasted_iota(jnp.int32, (rows, 128), 1)


def roll(v, shift):
    return pltpu.roll(v, shift, 1)


def shift_north(u, halo):
    left, right = u[:, :128], u[:, 128:]
    rl, rr = roll(left, 127), roll(right, 127)
    last = lane_iota(u.shape[0]) == 127
    return jnp.concatenate([jnp.where(last, rr, rl), jnp.where(last, halo, rr)], axis=1)


def shift_south(u, halo):
    left, right = u[:, :128], u[:, 128:]
    rl, rr = roll(left, 1), roll(right, 1)
    first = lane_iota(u.shape[0]) == 0
    return jnp.concatenate([jnp.where(first, halo, rl), jnp.where(first, rl, rr)], axis=1)


def signs(word, rows):
    bit = lax.broadcasted_iota(jnp.int32, (16, word.shape[1]), 0)
    spread = jnp.broadcast_to(word, (16, word.shape[1]))
    return (1 - 2 * jnp.bitwise_and(jnp.right_shift(spread, bit), 1)).astype(jnp.float32)


def kernel(
    sketch, words, ocean, east, north, kappa, area,
    image, gram,
    s, w_in, oc_in, co_in, cf, w_near, halo, sgn, pkg, in_pk, cor, in_cor, packN, packS, recN, recS,
    edge, edN, edS, fl, ret, out, mats, acc, pieces, rs, zb, ag,
    load_sem, small_sem, pkg_send, pkg_recv, cor_send, cor_recv, ret_send, ret_recv, near_send,
    near_recv, rounds, lat_send, lat_recv, lat2_send, lat2_recv, ar_send, ar_recv, store_sem,
):
    lon, lat = lax.axis_index("lon"), lax.axis_index("lat")
    c, zh = lax.rem(lon, 2), lax.rem(lon // 2, 2)
    y, x = lax.rem(lon // 4, 4), lon // 16
    z = zh * 8 + lat
    rank = (x * 4 + y) * 2 + c
    to_north = (lon, lat + 1)
    to_south = (lon, lat - 1)
    far_lon, near_lon = lax.rem(lon + 63 + 2 * c, 64), lon + 1 - 2 * c
    lat4 = lax.rem(lat + 4, 8)
    middle = (lax.rem(lon + 63 + c, 64), lat4)
    far_row, near_row = c * (I - 1), (1 - c) * (I - 1)
    by_far, by_near = 1 + (I - 3) * c, 1 + (I - 3) * (1 - c)

    def at_plane(dx, dy, dc):
        px, py, pc = lax.rem(x + dx, 4), lax.rem(y + dy, 4), lax.rem(c + dc, 2)
        return (px * 4 + py) * 2 + pc, device_at(px, py, z, pc)

    def at_line(d):
        return device_at(x, y, lax.rem(z + d, NZ), c)

    plane = [at_plane(*d) for d in STEPS]
    line = [at_line(d) for d in LINE]

    recN[...] = jnp.zeros((2, 16, 128), jnp.float32)
    recS[...] = jnp.zeros((2, 16, 128), jnp.float32)

    peers = [(far_lon, lat4)]
    peers += [at_line(d) for d in (4, NZ - 4)]
    peers += [at_plane(*d)[1] for d in ((2, 0, 0), (0, 2, 0))]
    peers += [at_line(d) for d in (1, NZ - 1)]
    peers += [at_plane(*d)[1] for d in ((1, 0, 0), (3, 0, 0), (0, 1, 0), (0, 3, 0), (0, 0, 1))]

    def tell(sem):
        for d in peers:
            pl.semaphore_signal(sem, inc=1, device_id=d, device_id_type=MESH)

    barrier = pltpu.get_barrier_semaphore()
    tell(barrier)

    def load_row(i):
        return pltpu.make_async_copy(sketch.at[:, i, :], s.at[i, pl.ds(0, SK), :], load_sem.at[i])

    small = [
        pltpu.make_async_copy(words, w_in, small_sem.at[0]),
        pltpu.make_async_copy(ocean, oc_in, small_sem.at[1]),
    ] + [
        pltpu.make_async_copy(a, co_in.at[k], small_sem.at[2 + k])
        for k, a in enumerate((east, north, kappa, area))
    ]
    order = [0, I - 1, 1, I - 2] + list(range(2, I - 2))
    for cp in small:
        cp.start()
    for i in order:
        load_row(i).start()
    for cp in small:
        cp.wait()

    sea = oc_in[...].astype(jnp.float32)
    for i in (0, I - 1):
        for w in range(2):
            s[i, pl.ds(EX + w, 1), :] = w_in[w, i : i + 1, :].astype(jnp.float32)
        s[i, pl.ds(EX + 2, 1), :] = sea[i : i + 1]
        s[i, pl.ds(EX + 3, 1), :] = co_in[0, i : i + 1, :]
        s[i, pl.ds(EX + 4, 1), :] = co_in[3, i : i + 1, :]
        s[i, pl.ds(EX + 5, 3), :] = jnp.zeros((3, J), jnp.float32)

    north_c, kap = co_in[1], co_in[2]
    beyond = jnp.zeros((I, 128), jnp.float32)
    w_n = north_c * sea * shift_north(sea, beyond)
    w_s = shift_south(w_n, beyond)
    inner_e = co_in[0, 0 : I - 1, :] * sea[0 : I - 1] * sea[1:I]
    cf[1, 0 : I - 1, :] = inner_e
    cf[1, I - 1 : I, :] = jnp.zeros((1, J), jnp.float32)
    cf[2, 1:I, :] = inner_e
    cf[2, 0:1, :] = jnp.zeros((1, J), jnp.float32)
    cf[3] = w_n
    cf[4] = w_s
    cf[0] = sea * (kap + cf[1] + cf[2] + w_n + w_s)
    cf[5] = co_in[3]
    cf[6] = jnp.sqrt(co_in[3])

    def own_signs(i, carry):
        for w in range(2):
            s[i, pl.ds(SG + 16 * w, 16), :] = signs(w_in[w, pl.ds(i, 1), :], 16)
        return carry

    lax.fori_loop(0, I, own_signs, 0)

    def rows_at(g):
        return pl.ds(16 * g if g < SK // 16 else SG + 16 * g - SK, 16)

    def weight(k, i):
        return cf[k, pl.ds(i, 1), :]

    for i in order[:4]:
        load_row(i).wait()
    w_inner = weight(1, (I - 2) * c)
    none = jnp.zeros((16, 128), jnp.float32)
    for g in range(NC // 16):
        here = s[far_row, rows_at(g), :]
        pkg[16 * g : 16 * g + 16, :] = (
            weight(0, far_row) * here
            - w_inner * s[by_far, rows_at(g), :]
            - weight(3, far_row) * shift_north(here, none)
            - weight(4, far_row) * shift_south(here, none)
        )
        if g < SK // 16:
            pkg[NC + 16 * g : NC + 16 * g + 16, :] = here
    pkg[PK:PKG, :] = s[far_row, pl.ds(EX, 8), :]

    def remote(src, dst, ss, rsem, d):
        return pltpu.make_async_remote_copy(
            src_ref=src, dst_ref=dst, send_sem=ss, recv_sem=rsem, device_id=d, device_id_type=MESH
        )

    def both_lats(turn):
        ss, rsem = ((lat_send, lat_recv), (lat2_send, lat2_recv))[turn]
        up = remote(packN, recS.at[turn], ss.at[0], rsem.at[0], to_north)
        down = remote(packS, recN.at[turn], ss.at[1], rsem.at[1], to_south)
        return up, down

    def start_lats(turn):
        up, down = both_lats(turn)
        pl.when(lat < 7)(up.start)
        pl.when(lat > 0)(down.start)

    def wait_lats(turn):
        up, down = both_lats(turn)

        @pl.when(lat < 7)
        def _():
            up.wait_send()
            down.wait_recv()

        @pl.when(lat > 0)
        def _():
            down.wait_send()
            up.wait_recv()

    def pack_edges(rows_of):
        edge[...] = jnp.zeros((2, SK, 128), jnp.float32)

        def step(i, carry):
            mine = lane_iota(8) == i
            for g in range(SK // 8):
                rows = pl.ds(8 * g, 8)
                v = rows_of(i, rows)
                edge[0, rows, :] = jnp.where(mine, roll(v[:, 128:], i + 1), edge[0, rows, :])
                edge[1, rows, :] = jnp.where(mine, roll(v[:, :128], i), edge[1, rows, :])
            return carry

        lax.fori_loop(0, I, step, 0)
        for side, pack in enumerate((packN, packS)):
            total = edge[side, 0:8, :]
            for g in range(1, SK // 8):
                total = total + roll(edge[side, 8 * g : 8 * g + 8, :], 16 * g)
            pack[0:8, :] = total

    for i in order[4:]:
        load_row(i).wait()

    w0f, w1f = w_in[0].astype(jnp.float32), w_in[1].astype(jnp.float32)
    sides = [a[:, h * 128 : h * 128 + 128] for h in (1, 0) for a in (w0f, w1f, sea, north_c)]
    turned = jnp.transpose(jnp.concatenate(sides, axis=0))
    packN[8:16, :] = jnp.broadcast_to(turned[127:128, :], (8, 128))
    packS[8:16, :] = jnp.broadcast_to(roll(turned[0:1, :], 64), (8, 128))
    pack_edges(lambda i, rows: s[i, rows, :])
    mats[...] = jnp.zeros(mats.shape, jnp.bfloat16)
    acc[...] = jnp.zeros(acc.shape, jnp.float32)

    pl.semaphore_wait(barrier, len(peers))

    start_lats(0)
    to_middle = remote(pkg, in_pk.at[1 - c], pkg_send, pkg_recv.at[1 - c], middle)
    to_middle.start()
    near = remote(
        s.at[near_row, pl.ds(0, MSG), :], halo, near_send.at[0], near_recv.at[0], (near_lon, lat)
    )
    near.start()
    tell(rounds.at[0])

    wait_lats(0)

    def column_of(rec):
        square = jnp.transpose(jnp.broadcast_to(rec[0, 8:9, :], (128, 128)))
        return square[32:48, :], square[48:64, :]

    def spread(turn, rec, ed):
        for g in range(SK // 8):
            v = rec[turn, 0:8, :]
            ed[8 * g : 8 * g + 8, :] = v if g == 0 else roll(v, 128 - 16 * g)

    def spread_signs(rec, ed):
        ints = rec[0, 8:9, :].astype(jnp.int32)
        for w in range(2):
            v = signs(ints, 16)
            ed[SK + 16 * w : SK + 16 * w + 16, :] = v if w == 0 else roll(v, 128 - 16)

    for rec, ed in ((recN, edN), (recS, edS)):
        spread(0, rec, ed)
        spread_signs(rec, ed)

    sea_n, _ = column_of(recN)
    sea_s, north_s = column_of(recS)
    w_n = north_c * sea * shift_north(sea, sea_n)
    w_s = shift_south(w_n, north_s * sea_s * sea[:, :128])
    cf[3] = w_n
    cf[4] = w_s
    cf[0] = sea * (kap + cf[1] + cf[2] + w_n + w_s)

    def halo_north(i, rows):
        return roll(edN[rows, :], 127 - i)

    def halo_south(i, rows):
        return roll(edS[rows, :], lax.rem(128 - i, 128))

    first, last = lane_iota(8) == 0, lane_iota(8) == 127
    total = jnp.zeros((8, 128), jnp.float32)
    wn_far, ws_far = weight(3, far_row), weight(4, far_row)
    for g in range(NC // 8):
        at = pl.ds(8 * g if g < SK // 8 else SG + 8 * g - SK, 8)
        rows = pl.ds(8 * g, 8)
        here = s[far_row, at, :]
        up = wn_far[:, 128:] * (here[:, 128:] - halo_north(far_row, rows))
        down = ws_far[:, :128] * (here[:, :128] - halo_south(far_row, rows))
        v = jnp.where(last, up, jnp.where(first, down, 0.0))
        total = total + (v if g == 0 else roll(v, 2 * g))
    cor[...] = total
    cor_to = remote(cor, in_cor.at[1 - c], cor_send, cor_recv.at[1 - c], middle)
    cor_to.start()

    pl.semaphore_wait(rounds.at[0], len(peers))
    tell(rounds.at[1])

    def stencil(i, here, across, erows):
        f = weight(0, i) * here
        for w, there in across:
            f = f - w * there
        return (
            f
            - weight(3, i) * shift_north(here, halo_north(i, erows))
            - weight(4, i) * shift_south(here, halo_south(i, erows))
        )

    def to_mats(slot, g, t):
        high = t.astype(jnp.bfloat16)
        mats[slot, pl.ds(16 * g, 16), :] = high
        mats[slot, pl.ds(128 + 16 * g, 16), :] = (t - high.astype(jnp.float32)).astype(jnp.bfloat16)

    def add_gram(slot):
        m = mats[slot]
        acc[...] += lax.dot_general(
            m, m, (((1,), (1,)), ((), ())), preferred_element_type=jnp.float32
        )

    def first_row(i, across):
        for g in range(NC // 16):
            f = stencil(i, s[i, rows_at(g), :], across(g), pl.ds(16 * g, 16))
            if g < SK // 16:
                fl[i + 1, pl.ds(16 * g, 16), :] = weight(5, i) * f
            to_mats(i, g, weight(6, i) * f)
        add_gram(i)

    def inner_first(i, carry):
        first_row(
            i,
            lambda g: (
                (weight(1, i), s[i + 1, rows_at(g), :]),
                (weight(2, i), s[i - 1, rows_at(g), :]),
            ),
        )
        return carry

    lax.fori_loop(1, I - 1, inner_first, 0)

    near.wait_recv()
    east_near = jnp.where(c == 1, halo[EX + 3 : EX + 4, :], co_in[0, I - 1 : I, :])
    w_near[...] = (
        east_near * halo[EX + 2 : EX + 3, :] * oc_in[pl.ds(near_row, 1), :].astype(jnp.float32)
    )
    cf[0, pl.ds(near_row, 1), :] += w_near[...] * oc_in[pl.ds(near_row, 1), :].astype(jnp.float32)
    for w in range(2):
        sgn[0, 16 * w : 16 * w + 16, :] = signs(halo[EX + w : EX + w + 1, :].astype(jnp.int32), 16)
    w_beside = weight(1, (I - 2) * (1 - c))

    def across_near(g):
        if g < SK // 16:
            there = halo[16 * g : 16 * g + 16, :]
        else:
            there = sgn[0, 16 * g - SK : 16 * g - SK + 16, :]
        return (w_near[...], there), (w_beside, s[by_near, rows_at(g), :])

    first_row(near_row, across_near)
    near2 = remote(
        fl.at[near_row + 1, pl.ds(0, SK), :], fl.at[c * (I + 1), pl.ds(0, SK), :],
        near_send.at[1], near_recv.at[1], (near_lon, lat),
    )
    near2.start()

    def ret_to(k):
        d = ((lon, lat4), (far_lon, lat4))[k]
        slot = (I, 0)[k]
        return remote(ret, fl.at[pl.ds(slot, 2)], ret_send.at[k], ret_recv, d)

    @pl.when(c == 1)
    def _():
        for k in range(2):
            remote(pkg, in_pk.at[k], pkg_send, pkg_recv.at[k], middle).wait_recv()
            remote(cor, in_cor.at[k], cor_send, cor_recv.at[k], middle).wait_recv()
        co = [[in_pk[k, PK + r : PK + r + 1, :] for r in range(5)] for k in range(2)]
        edge_w = co[0][3] * co[0][2] * co[1][2]
        roots = [jnp.sqrt(co[k][4]) for k in range(2)]
        ends = [lane_iota(8) == 0, lane_iota(8) == 127]
        for k in range(2):
            for w in range(2):
                sgn[k, 16 * w : 16 * w + 16, :] = signs(co[k][w].astype(jnp.int32), 16)
            ret[k, SK:RET, :] = jnp.broadcast_to(edge_w, (8, J))
        for g in range(NC // 16):
            if g < SK // 16:
                us = [in_pk[k, NC + 16 * g : NC + 16 * g + 16, :] for k in range(2)]
            else:
                us = [sgn[k, 16 * g - SK : 16 * g - SK + 16, :] for k in range(2)]
            d = edge_w * (us[0] - us[1])
            for k in range(2):
                fix = []
                for h in (2 * g, 2 * g + 1):
                    v = in_cor[k] if h == 0 else roll(in_cor[k], 128 - 2 * h)
                    fix.append(
                        jnp.concatenate([jnp.where(ends[n], v, 0.0) for n in range(2)], axis=1)
                    )
                f = in_pk[k, 16 * g : 16 * g + 16, :] + jnp.concatenate(fix, axis=0)
                f = f + d if k == 0 else f - d
                if g < SK // 16:
                    ret[k, 16 * g : 16 * g + 16, :] = co[k][4] * f
                to_mats(I - 1 + k, g, roots[k] * f)
        for k in range(2):
            ret_to(k).start()
        for k in range(2):
            add_gram(I - 1 + k)

    total = (acc[0:NC, 0:128] + acc[0:NC, 128:256]) + (
        acc[128 : 128 + NC, 0:128] + acc[128 : 128 + NC, 128:256]
    )
    for q in range(PLANE):
        pieces[q] = total[PIECE * q : PIECE * q + PIECE, :]
    pl.semaphore_wait(rounds.at[1], len(peers))
    for q, d in plane:
        remote(pieces.at[q], rs.at[rank], ar_send.at[0], ar_recv.at[0], d).start()
    rs[rank] = pieces[rank]

    def wait_all(ref, n, sem):
        pltpu.make_async_copy(ref.at[pl.ds(0, n)], ref.at[pl.ds(0, n)], sem).wait()

    wait_all(rs, PLANE - 1, ar_recv.at[0])
    zb[z] = jnp.sum(rs[...], axis=0)
    for d in line:
        remote(zb.at[z], zb.at[z], ar_send.at[1], ar_recv.at[1], d).start()
    wait_all(rs, PLANE - 1, ar_send.at[0])

    remote(ret, fl.at[pl.ds(I * c, 2)], ret_send.at[0], ret_recv, middle).wait_recv()
    near2.wait_recv()
    edge_w = fl[(I + 1) * c, SK : SK + 1, :]
    cf[1, I - 1 : I, :] = jnp.where(c == 1, edge_w, w_near[...])
    cf[2, 0:1, :] = jnp.where(c == 1, w_near[...], edge_w)
    cf[0, pl.ds(far_row, 1), :] += edge_w * oc_in[pl.ds(far_row, 1), :].astype(jnp.float32)
    pack_edges(lambda i, rows: fl[i + 1, rows, :])
    start_lats(1)
    wait_lats(1)
    for rec, ed in ((recN, edN), (recS, edS)):
        spread(1, rec, ed)

    def second_row(i, carry):
        for g in range(SK // 16):
            rows = pl.ds(16 * g, 16)
            across = (
                (weight(1, i), fl[i + 2, rows, :]),
                (weight(2, i), fl[i, rows, :]),
            )
            out[i, rows, :] = stencil(i, fl[i + 1, rows, :], across, rows)
        return carry

    lax.fori_loop(0, I, second_row, 0)

    def store_row(i):
        return pltpu.make_async_copy(out.at[i], image.at[:, i, :], store_sem.at[i])

    for i in range(I):
        store_row(i).start()

    wait_all(zb, NZ - 1, ar_recv.at[1])
    wait_all(zb, NZ - 1, ar_send.at[1])
    ag[rank] = jnp.sum(zb[...], axis=0) * (1.0 / CELLS)
    for _, d in plane:
        remote(ag.at[rank], ag.at[rank], ar_send.at[2], ar_recv.at[2], d).start()

    to_middle.wait_send()
    cor_to.wait_send()
    near.wait_send()
    near2.wait_send()

    @pl.when(c == 1)
    def _():
        for k in range(2):
            ret_to(k).wait_send()

    for i in range(I):
        store_row(i).wait()
    wait_all(ag, PLANE - 1, ar_recv.at[2])
    wait_all(ag, PLANE - 1, ar_send.at[2])
    for q in range(PLANE):
        gram[PIECE * q : PIECE * q + PIECE, :] = ag[q, :, 0:NC]


def local(sketch, probe_bits, ocean, east_cond, north_cond, kappa_sq, inv_area):
    f32 = jnp.float32

    def vmem(*shape, kind=f32):
        return pltpu.VMEM(shape, kind)

    dma = pltpu.SemaphoreType.DMA
    any_space = pl.BlockSpec(memory_space=pl.ANY)
    image, gram = pl.pallas_call(
        kernel,
        out_shape=(
            pltpu.VMEM((SK, I, J), f32),
            pltpu.VMEM((NC, NC), f32),
        ),
        in_specs=[pl.BlockSpec(memory_space=pltpu.HBM)] * 7,
        out_specs=(any_space, pl.BlockSpec(memory_space=pltpu.VMEM)),
        scratch_shapes=[
            vmem(I, ROWS, J),
            vmem(2, I, J, kind=jnp.int32),
            vmem(I, J, kind=jnp.int32),
            vmem(4, I, J),
            vmem(7, I, J),
            vmem(1, J),
            vmem(MSG, J),
            vmem(2, NP, J),
            vmem(PKG, J),
            vmem(2, PKG, J),
            vmem(8, 128),
            vmem(2, 8, 128),
            vmem(16, 128),
            vmem(16, 128),
            vmem(2, 16, 128),
            vmem(2, 16, 128),
            vmem(2, SK, 128),
            vmem(NC, 128),
            vmem(NC, 128),
            vmem(I + 2, RET, J),
            vmem(2, RET, J),
            vmem(I, SK, J),
            vmem(I + 1, 256, J, kind=jnp.bfloat16),
            vmem(256, 256),
            vmem(PLANE, PIECE, 128),
            vmem(PLANE, PIECE, 128),
            vmem(NZ, PIECE, 128),
            vmem(PLANE, PIECE, 128),
            dma((I,)),
            dma((6,)),
            dma,
            dma((2,)),
            dma,
            dma((2,)),
            dma((2,)),
            dma,
            dma((2,)),
            dma((2,)),
            pltpu.SemaphoreType.REGULAR((2,)),
            dma((2,)),
            dma((2,)),
            dma((2,)),
            dma((2,)),
            dma((3,)),
            dma((3,)),
            dma((I,)),
        ],
        compiler_params=pltpu.CompilerParams(
            collective_id=0, has_side_effects=True, vmem_limit_bytes=24 * 2**20
        ),
        name="nystrom",
    )(*[pltpu.with_memory_space_constraint(a, pltpu.HBM) for a in (sketch, probe_bits, ocean, east_cond, north_cond, kappa_sq, inv_area)])
    return image, gram


def solution(mesh):
    cells = P("lon", "lat")
    columns = P(None, "lon", "lat")
    return jax.shard_map(
        local,
        mesh=mesh,
        in_specs=(columns, columns, cells, cells, cells, cells, cells),
        out_specs=(columns, P()),
        check_vma=False,
    )
```

```python
import jax
import jax.numpy as jnp
from jax import lax
from jax.experimental import pallas as pl
from jax.experimental.pallas import tpu as pltpu
from jax.sharding import PartitionSpec as P

MESH = pl.DeviceIdType.MESH
SK = 64
NP = 32
NC = SK + NP
I = 16
J = 256
EX = SK
MSG = SK + 8
SG = MSG
ROWS = MSG + NP
PLANE = 32
NZ = 16
PIECE = NC // PLANE
CELLS = 2097152.0
PK = NC + SK
PKG = PK + 8
RET = SK + 8
STEPS = sorted(
    ((dx, dy, dc) for dx in range(4) for dy in range(4) for dc in range(2) if dx or dy or dc),
    key=lambda d: (-min(d[0], 4 - d[0]) - min(d[1], 4 - d[1]), -d[2]),
)
LINE = sorted(range(1, NZ), key=lambda d: -min(d, NZ - d))


def device_at(x, y, z, c):
    return (((x * 4 + y) * 2 + z // 8) * 2 + c, z % 8)


def lane_iota(rows):
    return lax.broadcasted_iota(jnp.int32, (rows, 128), 1)


def roll(v, shift):
    return pltpu.roll(v, shift, 1)


def shift_north(u, halo):
    left, right = u[:, :128], u[:, 128:]
    rl, rr = roll(left, 127), roll(right, 127)
    last = lane_iota(u.shape[0]) == 127
    return jnp.concatenate([jnp.where(last, rr, rl), jnp.where(last, halo, rr)], axis=1)


def shift_south(u, halo):
    left, right = u[:, :128], u[:, 128:]
    rl, rr = roll(left, 1), roll(right, 1)
    first = lane_iota(u.shape[0]) == 0
    return jnp.concatenate([jnp.where(first, halo, rl), jnp.where(first, rl, rr)], axis=1)


def signs(word, rows):
    bit = lax.broadcasted_iota(jnp.int32, (16, word.shape[1]), 0)
    spread = jnp.broadcast_to(word, (16, word.shape[1]))
    return (1 - 2 * jnp.bitwise_and(jnp.right_shift(spread, bit), 1)).astype(jnp.float32)


def kernel(
    sketch, words, ocean, east, north, kappa, area,
    image, gram,
    s, w_in, oc_in, co_in, cf, w_near, halo, sgn, pkg, in_pk, cor, in_cor, packN, packS, recN, recS,
    edN, edS, fl, ret, out, mats, acc, pieces, rs, zb, ag,
    load_sem, small_sem, pkg_send, pkg_recv, cor_send, cor_recv, ret_send, ret_recv, near_send,
    near_recv, rounds, lat_send, lat_recv, ar_send, ar_recv, store_sem,
):
    lon, lat = lax.axis_index("lon"), lax.axis_index("lat")
    c, zh = lax.rem(lon, 2), lax.rem(lon // 2, 2)
    y, x = lax.rem(lon // 4, 4), lon // 16
    z = zh * 8 + lat
    rank = (x * 4 + y) * 2 + c
    to_north = (lon, lat + 1)
    to_south = (lon, lat - 1)
    far_lon, near_lon = lax.rem(lon + 63 + 2 * c, 64), lon + 1 - 2 * c
    lat4 = lax.rem(lat + 4, 8)
    middle = (lax.rem(lon + 63 + c, 64), lat4)
    far_row, near_row = c * (I - 1), (1 - c) * (I - 1)
    by_far, by_near = 1 + (I - 3) * c, 1 + (I - 3) * (1 - c)

    def at_plane(dx, dy, dc):
        px, py, pc = lax.rem(x + dx, 4), lax.rem(y + dy, 4), lax.rem(c + dc, 2)
        return (px * 4 + py) * 2 + pc, device_at(px, py, z, pc)

    def at_line(d):
        return device_at(x, y, lax.rem(z + d, NZ), c)

    plane = [at_plane(*d) for d in STEPS]
    line = [at_line(d) for d in LINE]

    recN[...] = jnp.zeros((3, 16, 128), jnp.float32)
    recS[...] = jnp.zeros((3, 16, 128), jnp.float32)

    peers = [(far_lon, lat4)]
    peers += [at_line(d) for d in (4, NZ - 4)]
    peers += [at_plane(*d)[1] for d in ((2, 0, 0), (0, 2, 0))]
    peers += [at_line(d) for d in (1, NZ - 1)]
    peers += [at_plane(*d)[1] for d in ((1, 0, 0), (3, 0, 0), (0, 1, 0), (0, 3, 0), (0, 0, 1))]

    def tell(sem):
        for d in peers:
            pl.semaphore_signal(sem, inc=1, device_id=d, device_id_type=MESH)

    barrier = pltpu.get_barrier_semaphore()
    tell(barrier)

    def load_row(i):
        return pltpu.make_async_copy(sketch.at[:, i, :], s.at[i, pl.ds(0, SK), :], load_sem.at[i])

    small = [
        pltpu.make_async_copy(words, w_in, small_sem.at[0]),
        pltpu.make_async_copy(ocean, oc_in, small_sem.at[1]),
    ] + [
        pltpu.make_async_copy(a, co_in.at[k], small_sem.at[2 + k])
        for k, a in enumerate((east, north, kappa, area))
    ]
    order = [0, I - 1, 1, I - 2] + list(range(2, I - 2))
    for cp in small:
        cp.start()
    for i in order:
        load_row(i).start()
    for cp in small:
        cp.wait()

    sea = oc_in[...].astype(jnp.float32)
    for i in (0, I - 1):
        for w in range(2):
            s[i, pl.ds(EX + w, 1), :] = w_in[w, i : i + 1, :].astype(jnp.float32)
        s[i, pl.ds(EX + 2, 1), :] = sea[i : i + 1]
        s[i, pl.ds(EX + 3, 1), :] = co_in[0, i : i + 1, :]
        s[i, pl.ds(EX + 4, 1), :] = co_in[3, i : i + 1, :]
        s[i, pl.ds(EX + 5, 3), :] = jnp.zeros((3, J), jnp.float32)

    north_c, kap = co_in[1], co_in[2]
    beyond = jnp.zeros((I, 128), jnp.float32)
    w_n = north_c * sea * shift_north(sea, beyond)
    w_s = shift_south(w_n, beyond)
    inner_e = co_in[0, 0 : I - 1, :] * sea[0 : I - 1] * sea[1:I]
    cf[1, 0 : I - 1, :] = inner_e
    cf[1, I - 1 : I, :] = jnp.zeros((1, J), jnp.float32)
    cf[2, 1:I, :] = inner_e
    cf[2, 0:1, :] = jnp.zeros((1, J), jnp.float32)
    cf[3] = w_n
    cf[4] = w_s
    cf[0] = sea * (kap + cf[1] + cf[2] + w_n + w_s)
    cf[5] = co_in[3]
    cf[6] = jnp.sqrt(co_in[3])

    def own_signs(i, carry):
        for w in range(2):
            s[i, pl.ds(SG + 16 * w, 16), :] = signs(w_in[w, pl.ds(i, 1), :], 16)
        return carry

    own_signs(far_row, 0)
    own_signs(by_far, 0)

    def rows_at(g):
        return pl.ds(16 * g if g < SK // 16 else SG + 16 * g - SK, 16)

    def weight(k, i):
        return cf[k, pl.ds(i, 1), :]

    for i in order[:4]:
        load_row(i).wait()
    w_inner = weight(1, (I - 2) * c)
    none = jnp.zeros((16, 128), jnp.float32)
    for g in range(NC // 16):
        here = s[far_row, rows_at(g), :]
        pkg[16 * g : 16 * g + 16, :] = (
            weight(0, far_row) * here
            - w_inner * s[by_far, rows_at(g), :]
            - weight(3, far_row) * shift_north(here, none)
            - weight(4, far_row) * shift_south(here, none)
        )
        if g < SK // 16:
            pkg[NC + 16 * g : NC + 16 * g + 16, :] = here
    pkg[PK:PKG, :] = s[far_row, pl.ds(EX, 8), :]

    def remote(src, dst, ss, rsem, d):
        return pltpu.make_async_remote_copy(
            src_ref=src, dst_ref=dst, send_sem=ss, recv_sem=rsem, device_id=d, device_id_type=MESH
        )

    def both_lats(turn):
        rows = pl.ds(0, 8 if turn else 16)
        up = remote(
            packN.at[turn, rows], recS.at[turn, rows], lat_send.at[turn, 0],
            lat_recv.at[turn, 0], to_north,
        )
        down = remote(
            packS.at[turn, rows], recN.at[turn, rows], lat_send.at[turn, 1],
            lat_recv.at[turn, 1], to_south,
        )
        return up, down

    def start_lats(turn):
        up, down = both_lats(turn)
        pl.when(lat < 7)(up.start)
        pl.when(lat > 0)(down.start)

    def wait_lats(turn):
        up, down = both_lats(turn)

        @pl.when(lat < 7)
        def _():
            up.wait_send()
            down.wait_recv()

        @pl.when(lat > 0)
        def _():
            down.wait_send()
            up.wait_recv()

    def pack_edges(turn, rows_of, ids):
        lanes = lane_iota(8)
        totals = [[jnp.zeros((8, 128), jnp.float32) for _ in range(4)] for _ in range(2)]
        for g in range(SK // 8):
            for n, i in enumerate(ids):
                v = rows_of(i, pl.ds(8 * g, 8))
                for side, (u, shift) in enumerate(((v[:, 128:], 1), (v[:, :128], 0))):
                    by = 16 * g + i + shift
                    by = by % 128 if isinstance(i, int) else lax.rem(by, 128)
                    at = totals[side]
                    at[n % 4] = jnp.where(lanes == 16 * g + i, roll(u, by), at[n % 4])
        for side, pack in enumerate((packN, packS)):
            at = totals[side]
            pack[turn, 0:8, :] = (at[0] + at[1]) + (at[2] + at[3])

    pl.semaphore_wait(barrier, len(peers))

    to_middle = remote(pkg, in_pk.at[1 - c], pkg_send, pkg_recv.at[1 - c], middle)
    to_middle.start()
    near = remote(
        s.at[near_row, pl.ds(0, MSG), :], halo, near_send.at[0], near_recv.at[0], (near_lon, lat)
    )
    near.start()
    tell(rounds.at[0])

    for i in order[4:]:
        load_row(i).wait()

    w0f, w1f = w_in[0].astype(jnp.float32), w_in[1].astype(jnp.float32)
    sides = [a[:, h * 128 : h * 128 + 128] for h in (1, 0) for a in (w0f, w1f, sea, north_c)]
    turned = jnp.transpose(jnp.concatenate(sides, axis=0))
    packN[0, 8:16, :] = jnp.broadcast_to(turned[127:128, :], (8, 128))
    packS[0, 8:16, :] = jnp.broadcast_to(roll(turned[0:1, :], 64), (8, 128))
    pack_edges(0, lambda i, rows: s[i, rows, :], range(I))
    start_lats(0)

    lax.fori_loop(0, I, own_signs, 0)
    for at in (NC, 128 + NC):
        mats[:, at : at + 32, :] = jnp.zeros((I + 1, 32, J), jnp.bfloat16)
    acc[...] = jnp.zeros(acc.shape, jnp.float32)

    wait_lats(0)

    def column_of(rec):
        square = jnp.transpose(jnp.broadcast_to(rec[0, 8:9, :], (128, 128)))
        return square[32:48, :], square[48:64, :]

    def spread(v, ed):
        for g in range(SK // 8):
            ed[8 * g : 8 * g + 8, :] = v if g == 0 else roll(v, 128 - 16 * g)

    def spread_signs(rec, ed):
        ints = rec[0, 8:9, :].astype(jnp.int32)
        for w in range(2):
            v = signs(ints, 16)
            ed[SK + 16 * w : SK + 16 * w + 16, :] = v if w == 0 else roll(v, 128 - 16)

    for rec, ed in ((recN, edN), (recS, edS)):
        spread(rec[0, 0:8, :], ed)
        spread_signs(rec, ed)

    sea_n, _ = column_of(recN)
    sea_s, north_s = column_of(recS)
    w_n = north_c * sea * shift_north(sea, sea_n)
    w_s = shift_south(w_n, north_s * sea_s * sea[:, :128])
    cf[3] = w_n
    cf[4] = w_s
    cf[0] = sea * (kap + cf[1] + cf[2] + w_n + w_s)

    def halo_north(i, rows):
        return roll(edN[rows, :], 127 - i)

    def halo_south(i, rows):
        return roll(edS[rows, :], lax.rem(128 - i, 128))

    first, last = lane_iota(8) == 0, lane_iota(8) == 127
    total = jnp.zeros((8, 128), jnp.float32)
    wn_far, ws_far = weight(3, far_row), weight(4, far_row)
    for g in range(NC // 8):
        at = pl.ds(8 * g if g < SK // 8 else SG + 8 * g - SK, 8)
        rows = pl.ds(8 * g, 8)
        here = s[far_row, at, :]
        up = wn_far[:, 128:] * (here[:, 128:] - halo_north(far_row, rows))
        down = ws_far[:, :128] * (here[:, :128] - halo_south(far_row, rows))
        v = jnp.where(last, up, jnp.where(first, down, 0.0))
        total = total + (v if g == 0 else roll(v, 2 * g))
    cor[...] = total
    cor_to = remote(cor, in_cor.at[1 - c], cor_send, cor_recv.at[1 - c], middle)
    cor_to.start()

    pl.semaphore_wait(rounds.at[0], len(peers))
    tell(rounds.at[1])

    def stencil(i, here, across, erows):
        f = weight(0, i) * here
        for w, there in across:
            f = f - w * there
        return (
            f
            - weight(3, i) * shift_north(here, halo_north(i, erows))
            - weight(4, i) * shift_south(here, halo_south(i, erows))
        )

    def to_mats(slot, g, t):
        high = t.astype(jnp.bfloat16)
        mats[slot, pl.ds(16 * g, 16), :] = high
        mats[slot, pl.ds(128 + 16 * g, 16), :] = (t - high.astype(jnp.float32)).astype(jnp.bfloat16)

    def add_gram(slot):
        m = mats[slot]
        acc[...] += lax.dot_general(
            m, m, (((1,), (1,)), ((), ())), preferred_element_type=jnp.float32
        )

    def first_row(i, across):
        for g in range(NC // 16):
            f = stencil(i, s[i, rows_at(g), :], across(g), pl.ds(16 * g, 16))
            if g < SK // 16:
                fl[i + 1, pl.ds(16 * g, 16), :] = weight(5, i) * f
            to_mats(i, g, weight(6, i) * f)
        add_gram(i)

    def inner_first(i, carry):
        first_row(
            i,
            lambda g: (
                (weight(1, i), s[i + 1, rows_at(g), :]),
                (weight(2, i), s[i - 1, rows_at(g), :]),
            ),
        )
        return carry

    lax.fori_loop(1, I - 1, inner_first, 0)

    near.wait_recv()
    east_near = jnp.where(c == 1, halo[EX + 3 : EX + 4, :], co_in[0, I - 1 : I, :])
    w_near[...] = (
        east_near * halo[EX + 2 : EX + 3, :] * oc_in[pl.ds(near_row, 1), :].astype(jnp.float32)
    )
    cf[0, pl.ds(near_row, 1), :] += w_near[...] * oc_in[pl.ds(near_row, 1), :].astype(jnp.float32)
    for w in range(2):
        sgn[0, 16 * w : 16 * w + 16, :] = signs(halo[EX + w : EX + w + 1, :].astype(jnp.int32), 16)
    w_beside = weight(1, (I - 2) * (1 - c))

    def across_near(g):
        if g < SK // 16:
            there = halo[16 * g : 16 * g + 16, :]
        else:
            there = sgn[0, 16 * g - SK : 16 * g - SK + 16, :]
        return (w_near[...], there), (w_beside, s[by_near, rows_at(g), :])

    first_row(near_row, across_near)
    near2 = remote(
        fl.at[near_row + 1, pl.ds(0, SK), :], fl.at[c * (I + 1), pl.ds(0, SK), :],
        near_send.at[1], near_recv.at[1], (near_lon, lat),
    )
    near2.start()

    def ret_to(k):
        d = ((lon, lat4), (far_lon, lat4))[k]
        slot = (I, 0)[k]
        return remote(ret, fl.at[pl.ds(slot, 2)], ret_send.at[k], ret_recv, d)

    @pl.when(c == 1)
    def _():
        for k in range(2):
            remote(pkg, in_pk.at[k], pkg_send, pkg_recv.at[k], middle).wait_recv()
            remote(cor, in_cor.at[k], cor_send, cor_recv.at[k], middle).wait_recv()
        co = [[in_pk[k, PK + r : PK + r + 1, :] for r in range(5)] for k in range(2)]
        edge_w = co[0][3] * co[0][2] * co[1][2]
        roots = [jnp.sqrt(co[k][4]) for k in range(2)]
        ends = [lane_iota(8) == 0, lane_iota(8) == 127]
        for k in range(2):
            for w in range(2):
                sgn[k, 16 * w : 16 * w + 16, :] = signs(co[k][w].astype(jnp.int32), 16)
            ret[k, SK:RET, :] = jnp.broadcast_to(edge_w, (8, J))
        for g in range(NC // 16):
            if g < SK // 16:
                us = [in_pk[k, NC + 16 * g : NC + 16 * g + 16, :] for k in range(2)]
            else:
                us = [sgn[k, 16 * g - SK : 16 * g - SK + 16, :] for k in range(2)]
            d = edge_w * (us[0] - us[1])
            for k in range(2):
                fix = []
                for h in (2 * g, 2 * g + 1):
                    v = in_cor[k] if h == 0 else roll(in_cor[k], 128 - 2 * h)
                    fix.append(
                        jnp.concatenate([jnp.where(ends[n], v, 0.0) for n in range(2)], axis=1)
                    )
                f = in_pk[k, 16 * g : 16 * g + 16, :] + jnp.concatenate(fix, axis=0)
                f = f + d if k == 0 else f - d
                if g < SK // 16:
                    ret[k, 16 * g : 16 * g + 16, :] = co[k][4] * f
                to_mats(I - 1 + k, g, roots[k] * f)
        for k in range(2):
            ret_to(k).start()
        for k in range(2):
            add_gram(I - 1 + k)

    total = (acc[0:NC, 0:128] + acc[0:NC, 128:256]) + (
        acc[128 : 128 + NC, 0:128] + acc[128 : 128 + NC, 128:256]
    )
    for q in range(PLANE):
        pieces[q] = total[PIECE * q : PIECE * q + PIECE, :]
    pl.semaphore_wait(rounds.at[1], len(peers))
    for q, d in plane:
        remote(pieces.at[q], rs.at[rank], ar_send.at[0], ar_recv.at[0], d).start()
    rs[rank] = pieces[rank]

    def wait_all(ref, n, sem):
        pltpu.make_async_copy(ref.at[pl.ds(0, n)], ref.at[pl.ds(0, n)], sem).wait()

    def second_row(i, carry):
        for g in range(SK // 16):
            rows = pl.ds(16 * g, 16)
            across = (
                (weight(1, i), fl[i + 2, rows, :]),
                (weight(2, i), fl[i, rows, :]),
            )
            out[i, rows, :] = stencil(i, fl[i + 1, rows, :], across, rows)
        return carry

    def store_row(i):
        return pltpu.make_async_copy(out.at[i], image.at[:, i, :], store_sem.at[i])

    pack_edges(1, lambda i, rows: fl[i + 1, rows, :], list(range(1, I - 1)) + [near_row])
    start_lats(1)
    wait_lats(1)
    for rec, ed in ((recN, edN), (recS, edS)):
        spread(rec[1, 0:8, :], ed)
    lax.fori_loop(2, I - 2, second_row, 0)
    for i in range(2, I - 2):
        store_row(i).start()

    wait_all(rs, PLANE - 1, ar_recv.at[0])
    zb[z] = jnp.sum(rs[...], axis=0)
    for d in line:
        remote(zb.at[z], zb.at[z], ar_send.at[1], ar_recv.at[1], d).start()

    remote(ret, fl.at[pl.ds(I * c, 2)], ret_send.at[0], ret_recv, middle).wait_recv()
    pack_edges(2, lambda i, rows: fl[i + 1, rows, :], [far_row])
    start_lats(2)
    near2.wait_recv()
    edge_w = fl[(I + 1) * c, SK : SK + 1, :]
    cf[1, I - 1 : I, :] = jnp.where(c == 1, edge_w, w_near[...])
    cf[2, 0:1, :] = jnp.where(c == 1, w_near[...], edge_w)
    cf[0, pl.ds(far_row, 1), :] += edge_w * oc_in[pl.ds(far_row, 1), :].astype(jnp.float32)
    wait_lats(2)
    for rec, ed in ((recN, edN), (recS, edS)):
        spread(rec[1, 0:8, :] + rec[2, 0:8, :], ed)
    for i in (0, 1, I - 2, I - 1):
        second_row(i, 0)
        store_row(i).start()

    wait_all(zb, NZ - 1, ar_recv.at[1])
    ag[rank] = jnp.sum(zb[...], axis=0) * (1.0 / CELLS)
    for _, d in plane:
        remote(ag.at[rank], ag.at[rank], ar_send.at[2], ar_recv.at[2], d).start()

    wait_all(rs, PLANE - 1, ar_send.at[0])
    wait_all(zb, NZ - 1, ar_send.at[1])
    to_middle.wait_send()
    cor_to.wait_send()
    near.wait_send()
    near2.wait_send()

    @pl.when(c == 1)
    def _():
        for k in range(2):
            ret_to(k).wait_send()

    for i in range(I):
        store_row(i).wait()
    wait_all(ag, PLANE - 1, ar_recv.at[2])
    wait_all(ag, PLANE - 1, ar_send.at[2])
    for q in range(PLANE):
        gram[PIECE * q : PIECE * q + PIECE, :] = ag[q, :, 0:NC]


def finish(image, gram, image_out, gram_out, sems):
    copies = [pltpu.make_async_copy(gram, gram_out, sems.at[4])]
    for k in range(4):
        part = pl.ds(k * (SK // 4), SK // 4)
        copies.append(pltpu.make_async_copy(image.at[part], image_out.at[part], sems.at[k]))
    for copy in copies:
        copy.start()
    for copy in copies:
        copy.wait()


def local(sketch, probe_bits, ocean, east_cond, north_cond, kappa_sq, inv_area):
    f32 = jnp.float32

    def vmem(*shape, kind=f32):
        return pltpu.VMEM(shape, kind)

    dma = pltpu.SemaphoreType.DMA
    any_space = pl.BlockSpec(memory_space=pl.ANY)
    image, gram = pl.pallas_call(
        kernel,
        out_shape=(
            pltpu.VMEM((SK, I, J), f32),
            pltpu.VMEM((NC, NC), f32),
        ),
        in_specs=[pl.BlockSpec(memory_space=pltpu.HBM)] * 7,
        out_specs=(any_space, pl.BlockSpec(memory_space=pltpu.VMEM)),
        scratch_shapes=[
            vmem(I, ROWS, J),
            vmem(2, I, J, kind=jnp.int32),
            vmem(I, J, kind=jnp.int32),
            vmem(4, I, J),
            vmem(7, I, J),
            vmem(1, J),
            vmem(MSG, J),
            vmem(2, NP, J),
            vmem(PKG, J),
            vmem(2, PKG, J),
            vmem(8, 128),
            vmem(2, 8, 128),
            vmem(3, 16, 128),
            vmem(3, 16, 128),
            vmem(3, 16, 128),
            vmem(3, 16, 128),
            vmem(NC, 128),
            vmem(NC, 128),
            vmem(I + 2, RET, J),
            vmem(2, RET, J),
            vmem(I, SK, J),
            vmem(I + 1, 256, J, kind=jnp.bfloat16),
            vmem(256, 256),
            vmem(PLANE, PIECE, 128),
            vmem(PLANE, PIECE, 128),
            vmem(NZ, PIECE, 128),
            vmem(PLANE, PIECE, 128),
            dma((I,)),
            dma((6,)),
            dma,
            dma((2,)),
            dma,
            dma((2,)),
            dma((2,)),
            dma,
            dma((2,)),
            dma((2,)),
            pltpu.SemaphoreType.REGULAR((2,)),
            dma((3, 2)),
            dma((3, 2)),
            dma((3,)),
            dma((3,)),
            dma((I,)),
        ],
        compiler_params=pltpu.CompilerParams(
            collective_id=0, has_side_effects=True, vmem_limit_bytes=24 * 2**20
        ),
        name="nystrom",
    )(*[pltpu.with_memory_space_constraint(a, pltpu.HBM) for a in (sketch, probe_bits, ocean, east_cond, north_cond, kappa_sq, inv_area)])
    return pl.pallas_call(
        finish,
        out_shape=(
            jax.ShapeDtypeStruct((SK, I, J), f32),
            jax.ShapeDtypeStruct((NC, NC), f32),
        ),
        in_specs=[pl.BlockSpec(memory_space=pltpu.VMEM)] * 2,
        out_specs=(any_space, any_space),
        scratch_shapes=[dma((5,))],
        name="finish",
    )(*[pltpu.with_memory_space_constraint(a, pltpu.VMEM) for a in (image, gram)])


def solution(mesh):
    cells = P("lon", "lat")
    columns = P(None, "lon", "lat")
    return jax.shard_map(
        local,
        mesh=mesh,
        in_specs=(columns, columns, cells, cells, cells, cells, cells),
        out_specs=(columns, P()),
        check_vma=False,
    )
```

```python
import jax
import jax.numpy as jnp
from jax import lax
from jax.experimental import pallas as pl
from jax.experimental.pallas import tpu as pltpu
from jax.sharding import PartitionSpec as P

MESH = pl.DeviceIdType.MESH
SK = 64
NP = 32
NC = SK + NP
I = 16
J = 256
EX = SK
MSG = SK + 8
SG = MSG
ROWS = MSG + NP
PLANE = 32
NZ = 16
PIECE = NC // PLANE
CELLS = 2097152.0
PK = NC + SK
PKG = PK + 8
RET = SK + 8
STEPS = sorted(
    ((dx, dy, dc) for dx in range(4) for dy in range(4) for dc in range(2) if dx or dy or dc),
    key=lambda d: (-min(d[0], 4 - d[0]) - min(d[1], 4 - d[1]), -d[2]),
)
LINE = sorted(range(1, NZ), key=lambda d: -min(d, NZ - d))


def device_at(x, y, z, c):
    return (((x * 4 + y) * 2 + z // 8) * 2 + c, z % 8)


def lane_iota(rows):
    return lax.broadcasted_iota(jnp.int32, (rows, 128), 1)


def roll(v, shift):
    return pltpu.roll(v, shift, 1)


def shift_north(u, halo):
    left, right = u[:, :128], u[:, 128:]
    rl, rr = roll(left, 127), roll(right, 127)
    last = lane_iota(u.shape[0]) == 127
    return jnp.concatenate([jnp.where(last, rr, rl), jnp.where(last, halo, rr)], axis=1)


def shift_south(u, halo):
    left, right = u[:, :128], u[:, 128:]
    rl, rr = roll(left, 1), roll(right, 1)
    first = lane_iota(u.shape[0]) == 0
    return jnp.concatenate([jnp.where(first, halo, rl), jnp.where(first, rl, rr)], axis=1)


def signs(word, rows):
    bit = lax.broadcasted_iota(jnp.int32, (16, word.shape[1]), 0)
    spread = jnp.broadcast_to(word, (16, word.shape[1]))
    return (1 - 2 * jnp.bitwise_and(jnp.right_shift(spread, bit), 1)).astype(jnp.float32)


def kernel(
    sketch, words, ocean, east, north, kappa, area,
    image, gram,
    s, w_in, oc_in, co_in, cf, w_near, halo, sgn, pkg, in_pk, cor, in_cor, packN, packS, recN, recS,
    edN, edS, fl, ret, out, mats, acc, pieces, rs, zb, ag,
    load_sem, small_sem, pkg_send, pkg_recv, cor_send, cor_recv, ret_send, ret_recv, near_send,
    near_recv, rounds, lat_send, lat_recv, ar_send, ar_recv, store_sem,
):
    lon, lat = lax.axis_index("lon"), lax.axis_index("lat")
    c, zh = lax.rem(lon, 2), lax.rem(lon // 2, 2)
    y, x = lax.rem(lon // 4, 4), lon // 16
    z = zh * 8 + lat
    rank = (x * 4 + y) * 2 + c
    to_north = (lon, lat + 1)
    to_south = (lon, lat - 1)
    far_lon, near_lon = lax.rem(lon + 63 + 2 * c, 64), lon + 1 - 2 * c
    lat4 = lax.rem(lat + 4, 8)
    middle = (lax.rem(lon + 63 + c, 64), lat4)
    far_row, near_row = c * (I - 1), (1 - c) * (I - 1)
    by_far, by_near = 1 + (I - 3) * c, 1 + (I - 3) * (1 - c)

    def at_plane(dx, dy, dc):
        px, py, pc = lax.rem(x + dx, 4), lax.rem(y + dy, 4), lax.rem(c + dc, 2)
        return (px * 4 + py) * 2 + pc, device_at(px, py, z, pc)

    def at_line(d):
        return device_at(x, y, lax.rem(z + d, NZ), c)

    plane = [at_plane(*d) for d in STEPS]
    line = [at_line(d) for d in LINE]

    recN[...] = jnp.zeros((3, 16, 128), jnp.float32)
    recS[...] = jnp.zeros((3, 16, 128), jnp.float32)

    peers = [(far_lon, lat4)]
    peers += [at_line(d) for d in (4, NZ - 4)]
    peers += [at_plane(*d)[1] for d in ((2, 0, 0), (0, 2, 0))]
    peers += [at_line(d) for d in (1, NZ - 1)]
    peers += [at_plane(*d)[1] for d in ((1, 0, 0), (3, 0, 0), (0, 1, 0), (0, 3, 0), (0, 0, 1))]

    def tell(sem):
        for d in peers:
            pl.semaphore_signal(sem, inc=1, device_id=d, device_id_type=MESH)

    barrier = pltpu.get_barrier_semaphore()
    tell(barrier)

    def load_row(i):
        return pltpu.make_async_copy(sketch.at[:, i, :], s.at[i, pl.ds(0, SK), :], load_sem.at[i])

    small = [
        pltpu.make_async_copy(words, w_in, small_sem.at[0]),
        pltpu.make_async_copy(ocean, oc_in, small_sem.at[1]),
    ] + [
        pltpu.make_async_copy(a, co_in.at[k], small_sem.at[2 + k])
        for k, a in enumerate((east, north, kappa, area))
    ]
    order = [0, I - 1, 1, I - 2] + list(range(2, I - 2))
    for cp in small:
        cp.start()
    for i in order:
        load_row(i).start()
    for cp in small:
        cp.wait()

    sea = oc_in[...].astype(jnp.float32)
    for i in (0, I - 1):
        for w in range(2):
            s[i, pl.ds(EX + w, 1), :] = w_in[w, i : i + 1, :].astype(jnp.float32)
        s[i, pl.ds(EX + 2, 1), :] = sea[i : i + 1]
        s[i, pl.ds(EX + 3, 1), :] = co_in[0, i : i + 1, :]
        s[i, pl.ds(EX + 4, 1), :] = co_in[3, i : i + 1, :]
        s[i, pl.ds(EX + 5, 3), :] = jnp.zeros((3, J), jnp.float32)

    north_c, kap = co_in[1], co_in[2]
    beyond = jnp.zeros((I, 128), jnp.float32)
    w_n = north_c * sea * shift_north(sea, beyond)
    w_s = shift_south(w_n, beyond)
    inner_e = co_in[0, 0 : I - 1, :] * sea[0 : I - 1] * sea[1:I]
    cf[1, 0 : I - 1, :] = inner_e
    cf[1, I - 1 : I, :] = jnp.zeros((1, J), jnp.float32)
    cf[2, 1:I, :] = inner_e
    cf[2, 0:1, :] = jnp.zeros((1, J), jnp.float32)
    cf[3] = w_n
    cf[4] = w_s
    cf[0] = sea * (kap + cf[1] + cf[2] + w_n + w_s)
    cf[5] = co_in[3]
    cf[6] = jnp.sqrt(co_in[3])

    def own_signs(i, carry):
        for w in range(2):
            s[i, pl.ds(SG + 16 * w, 16), :] = signs(w_in[w, pl.ds(i, 1), :], 16)
        return carry

    own_signs(far_row, 0)
    own_signs(by_far, 0)

    def rows_at(g):
        return pl.ds(16 * g if g < SK // 16 else SG + 16 * g - SK, 16)

    def weight(k, i):
        return cf[k, pl.ds(i, 1), :]

    for i in order[:4]:
        load_row(i).wait()
    w_inner = weight(1, (I - 2) * c)
    none = jnp.zeros((16, 128), jnp.float32)
    for g in range(NC // 16):
        here = s[far_row, rows_at(g), :]
        pkg[16 * g : 16 * g + 16, :] = (
            weight(0, far_row) * here
            - w_inner * s[by_far, rows_at(g), :]
            - weight(3, far_row) * shift_north(here, none)
            - weight(4, far_row) * shift_south(here, none)
        )
        if g < SK // 16:
            pkg[NC + 16 * g : NC + 16 * g + 16, :] = here
    pkg[PK:PKG, :] = s[far_row, pl.ds(EX, 8), :]

    def remote(src, dst, ss, rsem, d):
        return pltpu.make_async_remote_copy(
            src_ref=src, dst_ref=dst, send_sem=ss, recv_sem=rsem, device_id=d, device_id_type=MESH
        )

    def both_lats(turn):
        rows = pl.ds(0, 8 if turn else 16)
        up = remote(
            packN.at[turn, rows], recS.at[turn, rows], lat_send.at[turn, 0],
            lat_recv.at[turn, 0], to_north,
        )
        down = remote(
            packS.at[turn, rows], recN.at[turn, rows], lat_send.at[turn, 1],
            lat_recv.at[turn, 1], to_south,
        )
        return up, down

    def start_lats(turn):
        up, down = both_lats(turn)
        pl.when(lat < 7)(up.start)
        pl.when(lat > 0)(down.start)

    def wait_lats(turn):
        up, down = both_lats(turn)

        @pl.when(lat < 7)
        def _():
            up.wait_send()
            down.wait_recv()

        @pl.when(lat > 0)
        def _():
            down.wait_send()
            up.wait_recv()

    def pack_edges(turn, rows_of, ids):
        lanes = lane_iota(8)
        totals = [[jnp.zeros((8, 128), jnp.float32) for _ in range(4)] for _ in range(2)]
        for g in range(SK // 8):
            for n, i in enumerate(ids):
                v = rows_of(i, pl.ds(8 * g, 8))
                for side, (u, shift) in enumerate(((v[:, 128:], 1), (v[:, :128], 0))):
                    by = 16 * g + i + shift
                    by = by % 128 if isinstance(i, int) else lax.rem(by, 128)
                    at = totals[side]
                    at[n % 4] = jnp.where(lanes == 16 * g + i, roll(u, by), at[n % 4])
        for side, pack in enumerate((packN, packS)):
            at = totals[side]
            pack[turn, 0:8, :] = (at[0] + at[1]) + (at[2] + at[3])

    for i in order[4:]:
        load_row(i).wait()

    w0f, w1f = w_in[0].astype(jnp.float32), w_in[1].astype(jnp.float32)
    sides = [a[:, h * 128 : h * 128 + 128] for h in (1, 0) for a in (w0f, w1f, sea, north_c)]
    turned = jnp.transpose(jnp.concatenate(sides, axis=0))
    packN[0, 8:16, :] = jnp.broadcast_to(turned[127:128, :], (8, 128))
    packS[0, 8:16, :] = jnp.broadcast_to(roll(turned[0:1, :], 64), (8, 128))
    pack_edges(0, lambda i, rows: s[i, rows, :], range(I))

    pl.semaphore_wait(barrier, len(peers))

    start_lats(0)
    to_middle = remote(pkg, in_pk.at[1 - c], pkg_send, pkg_recv.at[1 - c], middle)
    to_middle.start()
    near = remote(
        s.at[near_row, pl.ds(0, MSG), :], halo, near_send.at[0], near_recv.at[0], (near_lon, lat)
    )
    near.start()
    tell(rounds.at[0])

    lax.fori_loop(0, I, own_signs, 0)
    for at in (NC, 128 + NC):
        mats[:, at : at + 32, :] = jnp.zeros((I + 1, 32, J), jnp.bfloat16)
    acc[...] = jnp.zeros(acc.shape, jnp.float32)

    wait_lats(0)

    def column_of(rec):
        square = jnp.transpose(jnp.broadcast_to(rec[0, 8:9, :], (128, 128)))
        return square[32:48, :], square[48:64, :]

    def spread(v, ed):
        for g in range(SK // 8):
            ed[8 * g : 8 * g + 8, :] = v if g == 0 else roll(v, 128 - 16 * g)

    def spread_signs(rec, ed):
        ints = rec[0, 8:9, :].astype(jnp.int32)
        for w in range(2):
            v = signs(ints, 16)
            ed[SK + 16 * w : SK + 16 * w + 16, :] = v if w == 0 else roll(v, 128 - 16)

    for rec, ed in ((recN, edN), (recS, edS)):
        spread(rec[0, 0:8, :], ed)
        spread_signs(rec, ed)

    sea_n, _ = column_of(recN)
    sea_s, north_s = column_of(recS)
    w_n = north_c * sea * shift_north(sea, sea_n)
    w_s = shift_south(w_n, north_s * sea_s * sea[:, :128])
    cf[3] = w_n
    cf[4] = w_s
    cf[0] = sea * (kap + cf[1] + cf[2] + w_n + w_s)

    def halo_north(i, rows):
        return roll(edN[rows, :], 127 - i)

    def halo_south(i, rows):
        return roll(edS[rows, :], lax.rem(128 - i, 128))

    first, last = lane_iota(8) == 0, lane_iota(8) == 127
    total = jnp.zeros((8, 128), jnp.float32)
    wn_far, ws_far = weight(3, far_row), weight(4, far_row)
    for g in range(NC // 8):
        at = pl.ds(8 * g if g < SK // 8 else SG + 8 * g - SK, 8)
        rows = pl.ds(8 * g, 8)
        here = s[far_row, at, :]
        up = wn_far[:, 128:] * (here[:, 128:] - halo_north(far_row, rows))
        down = ws_far[:, :128] * (here[:, :128] - halo_south(far_row, rows))
        v = jnp.where(last, up, jnp.where(first, down, 0.0))
        total = total + (v if g == 0 else roll(v, 2 * g))
    cor[...] = total
    cor_to = remote(cor, in_cor.at[1 - c], cor_send, cor_recv.at[1 - c], middle)
    cor_to.start()

    pl.semaphore_wait(rounds.at[0], len(peers))
    tell(rounds.at[1])

    def stencil(i, here, across, erows):
        f = weight(0, i) * here
        for w, there in across:
            f = f - w * there
        return (
            f
            - weight(3, i) * shift_north(here, halo_north(i, erows))
            - weight(4, i) * shift_south(here, halo_south(i, erows))
        )

    def to_mats(slot, g, t):
        high = t.astype(jnp.bfloat16)
        mats[slot, pl.ds(16 * g, 16), :] = high
        mats[slot, pl.ds(128 + 16 * g, 16), :] = (t - high.astype(jnp.float32)).astype(jnp.bfloat16)

    def add_gram(slot):
        m = mats[slot]
        acc[...] += lax.dot_general(
            m, m, (((1,), (1,)), ((), ())), preferred_element_type=jnp.float32
        )

    def first_row(i, across):
        for g in range(NC // 16):
            f = stencil(i, s[i, rows_at(g), :], across(g), pl.ds(16 * g, 16))
            if g < SK // 16:
                fl[i + 1, pl.ds(16 * g, 16), :] = weight(5, i) * f
            to_mats(i, g, weight(6, i) * f)
        add_gram(i)

    def inner_first(i, carry):
        first_row(
            i,
            lambda g: (
                (weight(1, i), s[i + 1, rows_at(g), :]),
                (weight(2, i), s[i - 1, rows_at(g), :]),
            ),
        )
        return carry

    lax.fori_loop(1, I - 1, inner_first, 0)

    near.wait_recv()
    east_near = jnp.where(c == 1, halo[EX + 3 : EX + 4, :], co_in[0, I - 1 : I, :])
    w_near[...] = (
        east_near * halo[EX + 2 : EX + 3, :] * oc_in[pl.ds(near_row, 1), :].astype(jnp.float32)
    )
    cf[0, pl.ds(near_row, 1), :] += w_near[...] * oc_in[pl.ds(near_row, 1), :].astype(jnp.float32)
    for w in range(2):
        sgn[0, 16 * w : 16 * w + 16, :] = signs(halo[EX + w : EX + w + 1, :].astype(jnp.int32), 16)
    w_beside = weight(1, (I - 2) * (1 - c))

    def across_near(g):
        if g < SK // 16:
            there = halo[16 * g : 16 * g + 16, :]
        else:
            there = sgn[0, 16 * g - SK : 16 * g - SK + 16, :]
        return (w_near[...], there), (w_beside, s[by_near, rows_at(g), :])

    first_row(near_row, across_near)
    near2 = remote(
        fl.at[near_row + 1, pl.ds(0, SK), :], fl.at[c * (I + 1), pl.ds(0, SK), :],
        near_send.at[1], near_recv.at[1], (near_lon, lat),
    )
    near2.start()

    def ret_to(k):
        d = ((lon, lat4), (far_lon, lat4))[k]
        slot = (I, 0)[k]
        return remote(ret, fl.at[pl.ds(slot, 2)], ret_send.at[k], ret_recv, d)

    @pl.when(c == 1)
    def _():
        for k in range(2):
            remote(pkg, in_pk.at[k], pkg_send, pkg_recv.at[k], middle).wait_recv()
            remote(cor, in_cor.at[k], cor_send, cor_recv.at[k], middle).wait_recv()
        co = [[in_pk[k, PK + r : PK + r + 1, :] for r in range(5)] for k in range(2)]
        edge_w = co[0][3] * co[0][2] * co[1][2]
        roots = [jnp.sqrt(co[k][4]) for k in range(2)]
        ends = [lane_iota(8) == 0, lane_iota(8) == 127]
        for k in range(2):
            for w in range(2):
                sgn[k, 16 * w : 16 * w + 16, :] = signs(co[k][w].astype(jnp.int32), 16)
            ret[k, SK:RET, :] = jnp.broadcast_to(edge_w, (8, J))
        for g in range(NC // 16):
            if g < SK // 16:
                us = [in_pk[k, NC + 16 * g : NC + 16 * g + 16, :] for k in range(2)]
            else:
                us = [sgn[k, 16 * g - SK : 16 * g - SK + 16, :] for k in range(2)]
            d = edge_w * (us[0] - us[1])
            for k in range(2):
                fix = []
                for h in (2 * g, 2 * g + 1):
                    v = in_cor[k] if h == 0 else roll(in_cor[k], 128 - 2 * h)
                    fix.append(
                        jnp.concatenate([jnp.where(ends[n], v, 0.0) for n in range(2)], axis=1)
                    )
                f = in_pk[k, 16 * g : 16 * g + 16, :] + jnp.concatenate(fix, axis=0)
                f = f + d if k == 0 else f - d
                if g < SK // 16:
                    ret[k, 16 * g : 16 * g + 16, :] = co[k][4] * f
                to_mats(I - 1 + k, g, roots[k] * f)
        for k in range(2):
            add_gram(I - 1 + k)

    total = (acc[0:NC, 0:128] + acc[0:NC, 128:256]) + (
        acc[128 : 128 + NC, 0:128] + acc[128 : 128 + NC, 128:256]
    )
    for q in range(PLANE):
        pieces[q] = total[PIECE * q : PIECE * q + PIECE, :]
    pl.semaphore_wait(rounds.at[1], len(peers))
    for q, d in plane:
        remote(pieces.at[q], rs.at[rank], ar_send.at[0], ar_recv.at[0], d).start()
    rs[rank] = pieces[rank]

    def wait_all(ref, n, sem):
        pltpu.make_async_copy(ref.at[pl.ds(0, n)], ref.at[pl.ds(0, n)], sem).wait()

    def second_row(i, carry):
        for g in range(SK // 16):
            rows = pl.ds(16 * g, 16)
            across = (
                (weight(1, i), fl[i + 2, rows, :]),
                (weight(2, i), fl[i, rows, :]),
            )
            out[i, rows, :] = stencil(i, fl[i + 1, rows, :], across, rows)
        return carry

    def store_row(i):
        return pltpu.make_async_copy(out.at[i], image.at[:, i, :], store_sem.at[i])

    pack_edges(1, lambda i, rows: fl[i + 1, rows, :], list(range(1, I - 1)) + [near_row])
    start_lats(1)
    wait_lats(1)
    for rec, ed in ((recN, edN), (recS, edS)):
        spread(rec[1, 0:8, :], ed)
    lax.fori_loop(2, I - 2, second_row, 0)
    for i in range(2, I - 2):
        store_row(i).start()

    wait_all(rs, PLANE - 1, ar_recv.at[0])
    zb[z] = jnp.sum(rs[...], axis=0)
    for d in line:
        remote(zb.at[z], zb.at[z], ar_send.at[1], ar_recv.at[1], d).start()

    @pl.when(c == 1)
    def _():
        for k in range(2):
            ret_to(k).start()

    wait_all(zb, NZ - 1, ar_recv.at[1])
    ag[rank] = jnp.sum(zb[...], axis=0) * (1.0 / CELLS)
    for _, d in plane:
        remote(ag.at[rank], ag.at[rank], ar_send.at[2], ar_recv.at[2], d).start()

    remote(ret, fl.at[pl.ds(I * c, 2)], ret_send.at[0], ret_recv, middle).wait_recv()
    pack_edges(2, lambda i, rows: fl[i + 1, rows, :], [far_row])
    start_lats(2)
    near2.wait_recv()
    edge_w = fl[(I + 1) * c, SK : SK + 1, :]
    cf[1, I - 1 : I, :] = jnp.where(c == 1, edge_w, w_near[...])
    cf[2, 0:1, :] = jnp.where(c == 1, w_near[...], edge_w)
    cf[0, pl.ds(far_row, 1), :] += edge_w * oc_in[pl.ds(far_row, 1), :].astype(jnp.float32)
    wait_lats(2)
    for rec, ed in ((recN, edN), (recS, edS)):
        spread(rec[1, 0:8, :] + rec[2, 0:8, :], ed)
    for i in (0, 1, I - 2, I - 1):
        second_row(i, 0)
        store_row(i).start()

    wait_all(rs, PLANE - 1, ar_send.at[0])
    wait_all(zb, NZ - 1, ar_send.at[1])
    to_middle.wait_send()
    cor_to.wait_send()
    near.wait_send()
    near2.wait_send()

    @pl.when(c == 1)
    def _():
        for k in range(2):
            ret_to(k).wait_send()

    for i in range(I):
        store_row(i).wait()
    wait_all(ag, PLANE - 1, ar_recv.at[2])
    wait_all(ag, PLANE - 1, ar_send.at[2])
    for q in range(PLANE):
        gram[PIECE * q : PIECE * q + PIECE, :] = ag[q, :, 0:NC]


def finish(image, gram, image_out, gram_out, sems):
    copies = [pltpu.make_async_copy(gram, gram_out, sems.at[4])]
    for k in range(4):
        part = pl.ds(k * (SK // 4), SK // 4)
        copies.append(pltpu.make_async_copy(image.at[part], image_out.at[part], sems.at[k]))
    for copy in copies:
        copy.start()
    for copy in copies:
        copy.wait()


def local(sketch, probe_bits, ocean, east_cond, north_cond, kappa_sq, inv_area):
    f32 = jnp.float32

    def vmem(*shape, kind=f32):
        return pltpu.VMEM(shape, kind)

    dma = pltpu.SemaphoreType.DMA
    any_space = pl.BlockSpec(memory_space=pl.ANY)
    image, gram = pl.pallas_call(
        kernel,
        out_shape=(
            pltpu.VMEM((SK, I, J), f32),
            pltpu.VMEM((NC, NC), f32),
        ),
        in_specs=[pl.BlockSpec(memory_space=pltpu.HBM)] * 7,
        out_specs=(any_space, pl.BlockSpec(memory_space=pltpu.VMEM)),
        scratch_shapes=[
            vmem(I, ROWS, J),
            vmem(2, I, J, kind=jnp.int32),
            vmem(I, J, kind=jnp.int32),
            vmem(4, I, J),
            vmem(7, I, J),
            vmem(1, J),
            vmem(MSG, J),
            vmem(2, NP, J),
            vmem(PKG, J),
            vmem(2, PKG, J),
            vmem(8, 128),
            vmem(2, 8, 128),
            vmem(3, 16, 128),
            vmem(3, 16, 128),
            vmem(3, 16, 128),
            vmem(3, 16, 128),
            vmem(NC, 128),
            vmem(NC, 128),
            vmem(I + 2, RET, J),
            vmem(2, RET, J),
            vmem(I, SK, J),
            vmem(I + 1, 256, J, kind=jnp.bfloat16),
            vmem(256, 256),
            vmem(PLANE, PIECE, 128),
            vmem(PLANE, PIECE, 128),
            vmem(NZ, PIECE, 128),
            vmem(PLANE, PIECE, 128),
            dma((I,)),
            dma((6,)),
            dma,
            dma((2,)),
            dma,
            dma((2,)),
            dma((2,)),
            dma,
            dma((2,)),
            dma((2,)),
            pltpu.SemaphoreType.REGULAR((2,)),
            dma((3, 2)),
            dma((3, 2)),
            dma((3,)),
            dma((3,)),
            dma((I,)),
        ],
        compiler_params=pltpu.CompilerParams(
            collective_id=0, has_side_effects=True, vmem_limit_bytes=24 * 2**20
        ),
        name="nystrom",
    )(*[pltpu.with_memory_space_constraint(a, pltpu.HBM) for a in (sketch, probe_bits, ocean, east_cond, north_cond, kappa_sq, inv_area)])
    return pl.pallas_call(
        finish,
        out_shape=(
            jax.ShapeDtypeStruct((SK, I, J), f32),
            jax.ShapeDtypeStruct((NC, NC), f32),
        ),
        in_specs=[pl.BlockSpec(memory_space=pltpu.VMEM)] * 2,
        out_specs=(any_space, any_space),
        scratch_shapes=[dma((5,))],
        name="finish",
    )(*[pltpu.with_memory_space_constraint(a, pltpu.VMEM) for a in (image, gram)])


def solution(mesh):
    cells = P("lon", "lat")
    columns = P(None, "lon", "lat")
    return jax.shard_map(
        local,
        mesh=mesh,
        in_specs=(columns, columns, cells, cells, cells, cells, cells),
        out_specs=(columns, P()),
        check_vma=False,
    )
```

```python
import jax
import jax.numpy as jnp
from jax import lax
from jax.experimental import pallas as pl
from jax.experimental.pallas import tpu as pltpu
from jax.sharding import PartitionSpec as P

MESH = pl.DeviceIdType.MESH
SK = 64
NP = 32
NC = SK + NP
I = 16
J = 256
EX = SK
MSG = SK + 8
SG = MSG
ROWS = MSG + NP
PLANE = 32
NZ = 16
PIECE = NC // PLANE
CELLS = 2097152.0
PK = NC + SK
PKG = PK + 8
RET = SK + 8
STEPS = sorted(
    ((dx, dy, dc) for dx in range(4) for dy in range(4) for dc in range(2) if dx or dy or dc),
    key=lambda d: (-min(d[0], 4 - d[0]) - min(d[1], 4 - d[1]), -d[2]),
)
LINE = sorted(range(1, NZ), key=lambda d: -min(d, NZ - d))


def device_at(x, y, z, c):
    return (((x * 4 + y) * 2 + z // 8) * 2 + c, z % 8)


def lane_iota(rows):
    return lax.broadcasted_iota(jnp.int32, (rows, 128), 1)


def roll(v, shift):
    return pltpu.roll(v, shift, 1)


def shift_north(u, halo):
    left, right = u[:, :128], u[:, 128:]
    rl, rr = roll(left, 127), roll(right, 127)
    last = lane_iota(u.shape[0]) == 127
    return jnp.concatenate([jnp.where(last, rr, rl), jnp.where(last, halo, rr)], axis=1)


def shift_south(u, halo):
    left, right = u[:, :128], u[:, 128:]
    rl, rr = roll(left, 1), roll(right, 1)
    first = lane_iota(u.shape[0]) == 0
    return jnp.concatenate([jnp.where(first, halo, rl), jnp.where(first, rl, rr)], axis=1)


def signs(word, rows):
    bit = lax.broadcasted_iota(jnp.int32, (16, word.shape[1]), 0)
    spread = jnp.broadcast_to(word, (16, word.shape[1]))
    return (1 - 2 * jnp.bitwise_and(jnp.right_shift(spread, bit), 1)).astype(jnp.float32)


def kernel(
    sketch, words, ocean, east, north, kappa, area,
    image, gram,
    s, w_in, oc_in, co_in, cf, w_near, halo, sgn, pkg, in_pk, cor, in_cor, packN, packS, recN, recS,
    edN, edS, fl, ret, out, mats, acc, pieces, rs, zb, ag,
    load_sem, small_sem, pkg_send, pkg_recv, cor_send, cor_recv, ret_send, ret_recv, near_send,
    near_recv, rounds, lat_send, lat_recv, ar_send, ar_recv, store_sem,
):
    lon, lat = lax.axis_index("lon"), lax.axis_index("lat")
    c, zh = lax.rem(lon, 2), lax.rem(lon // 2, 2)
    y, x = lax.rem(lon // 4, 4), lon // 16
    z = zh * 8 + lat
    rank = (x * 4 + y) * 2 + c
    to_north = (lon, lat + 1)
    to_south = (lon, lat - 1)
    far_lon, near_lon = lax.rem(lon + 63 + 2 * c, 64), lon + 1 - 2 * c
    lat4 = lax.rem(lat + 4, 8)
    middle = (lax.rem(lon + 63 + c, 64), lat4)
    far_row, near_row = c * (I - 1), (1 - c) * (I - 1)
    by_far, by_near = 1 + (I - 3) * c, 1 + (I - 3) * (1 - c)

    def at_plane(dx, dy, dc):
        px, py, pc = lax.rem(x + dx, 4), lax.rem(y + dy, 4), lax.rem(c + dc, 2)
        return (px * 4 + py) * 2 + pc, device_at(px, py, z, pc)

    def at_line(d):
        return device_at(x, y, lax.rem(z + d, NZ), c)

    plane = [at_plane(*d) for d in STEPS]
    line = [at_line(d) for d in LINE]

    recN[...] = jnp.zeros((3, 16, 128), jnp.float32)
    recS[...] = jnp.zeros((3, 16, 128), jnp.float32)

    peers = [(far_lon, lat4)]
    peers += [at_line(d) for d in (4, NZ - 4)]
    peers += [at_plane(*d)[1] for d in ((2, 0, 0), (0, 2, 0))]
    peers += [at_line(d) for d in (1, NZ - 1)]
    peers += [at_plane(*d)[1] for d in ((1, 0, 0), (3, 0, 0), (0, 1, 0), (0, 3, 0), (0, 0, 1))]

    def tell(sem):
        for d in peers:
            pl.semaphore_signal(sem, inc=1, device_id=d, device_id_type=MESH)

    barrier = pltpu.get_barrier_semaphore()
    tell(barrier)

    def load_row(i):
        return pltpu.make_async_copy(sketch.at[:, i, :], s.at[i, pl.ds(0, SK), :], load_sem.at[i])

    small = [
        pltpu.make_async_copy(words, w_in, small_sem.at[0]),
        pltpu.make_async_copy(ocean, oc_in, small_sem.at[1]),
    ] + [
        pltpu.make_async_copy(a, co_in.at[k], small_sem.at[2 + k])
        for k, a in enumerate((east, north, kappa, area))
    ]
    order = [0, I - 1, 1, I - 2] + list(range(2, I - 2))
    for cp in small:
        cp.start()
    for i in order:
        load_row(i).start()
    for cp in small:
        cp.wait()

    sea = oc_in[...].astype(jnp.float32)
    for i in (0, I - 1):
        for w in range(2):
            s[i, pl.ds(EX + w, 1), :] = w_in[w, i : i + 1, :].astype(jnp.float32)
        s[i, pl.ds(EX + 2, 1), :] = sea[i : i + 1]
        s[i, pl.ds(EX + 3, 1), :] = co_in[0, i : i + 1, :]
        s[i, pl.ds(EX + 4, 1), :] = co_in[3, i : i + 1, :]
        s[i, pl.ds(EX + 5, 3), :] = jnp.zeros((3, J), jnp.float32)

    north_c, kap = co_in[1], co_in[2]
    beyond = jnp.zeros((I, 128), jnp.float32)
    w_n = north_c * sea * shift_north(sea, beyond)
    w_s = shift_south(w_n, beyond)
    inner_e = co_in[0, 0 : I - 1, :] * sea[0 : I - 1] * sea[1:I]
    cf[1, 0 : I - 1, :] = inner_e
    cf[1, I - 1 : I, :] = jnp.zeros((1, J), jnp.float32)
    cf[2, 1:I, :] = inner_e
    cf[2, 0:1, :] = jnp.zeros((1, J), jnp.float32)
    cf[3] = w_n
    cf[4] = w_s
    cf[0] = sea * (kap + cf[1] + cf[2] + w_n + w_s)
    cf[5] = co_in[3]
    cf[6] = jnp.sqrt(co_in[3])

    def own_signs(i, carry):
        for w in range(2):
            s[i, pl.ds(SG + 16 * w, 16), :] = signs(w_in[w, pl.ds(i, 1), :], 16)
        return carry

    own_signs(far_row, 0)
    own_signs(by_far, 0)

    def rows_at(g):
        return pl.ds(16 * g if g < SK // 16 else SG + 16 * g - SK, 16)

    def weight(k, i):
        return cf[k, pl.ds(i, 1), :]

    for i in order[:4]:
        load_row(i).wait()
    w_inner = weight(1, (I - 2) * c)
    none = jnp.zeros((16, 128), jnp.float32)
    for g in range(NC // 16):
        here = s[far_row, rows_at(g), :]
        pkg[16 * g : 16 * g + 16, :] = (
            weight(0, far_row) * here
            - w_inner * s[by_far, rows_at(g), :]
            - weight(3, far_row) * shift_north(here, none)
            - weight(4, far_row) * shift_south(here, none)
        )
        if g < SK // 16:
            pkg[NC + 16 * g : NC + 16 * g + 16, :] = here
    pkg[PK:PKG, :] = s[far_row, pl.ds(EX, 8), :]

    def remote(src, dst, ss, rsem, d):
        return pltpu.make_async_remote_copy(
            src_ref=src, dst_ref=dst, send_sem=ss, recv_sem=rsem, device_id=d, device_id_type=MESH
        )

    def both_lats(turn):
        rows = pl.ds(0, 8 if turn else 16)
        up = remote(
            packN.at[turn, rows], recS.at[turn, rows], lat_send.at[turn, 0],
            lat_recv.at[turn, 0], to_north,
        )
        down = remote(
            packS.at[turn, rows], recN.at[turn, rows], lat_send.at[turn, 1],
            lat_recv.at[turn, 1], to_south,
        )
        return up, down

    def start_lats(turn):
        up, down = both_lats(turn)
        pl.when(lat < 7)(up.start)
        pl.when(lat > 0)(down.start)

    def wait_lats(turn):
        up, down = both_lats(turn)

        @pl.when(lat < 7)
        def _():
            up.wait_send()
            down.wait_recv()

        @pl.when(lat > 0)
        def _():
            down.wait_send()
            up.wait_recv()

    def pack_edges(turn, rows_of, ids):
        lanes = lane_iota(8)
        totals = [[jnp.zeros((8, 128), jnp.float32) for _ in range(4)] for _ in range(2)]
        for g in range(SK // 8):
            for n, i in enumerate(ids):
                v = rows_of(i, pl.ds(8 * g, 8))
                for side, (u, shift) in enumerate(((v[:, 128:], 1), (v[:, :128], 0))):
                    by = 16 * g + i + shift
                    by = by % 128 if isinstance(i, int) else lax.rem(by, 128)
                    at = totals[side]
                    at[n % 4] = jnp.where(lanes == 16 * g + i, roll(u, by), at[n % 4])
        for side, pack in enumerate((packN, packS)):
            at = totals[side]
            pack[turn, 0:8, :] = (at[0] + at[1]) + (at[2] + at[3])

    for i in order[4:]:
        load_row(i).wait()

    w0f, w1f = w_in[0].astype(jnp.float32), w_in[1].astype(jnp.float32)
    sides = [a[:, h * 128 : h * 128 + 128] for h in (1, 0) for a in (w0f, w1f, sea, north_c)]
    turned = jnp.transpose(jnp.concatenate(sides, axis=0))
    packN[0, 8:16, :] = jnp.broadcast_to(turned[127:128, :], (8, 128))
    packS[0, 8:16, :] = jnp.broadcast_to(roll(turned[0:1, :], 64), (8, 128))
    pack_edges(0, lambda i, rows: s[i, rows, :], range(I))

    pl.semaphore_wait(barrier, len(peers))

    start_lats(0)
    to_middle = remote(pkg, in_pk.at[1 - c], pkg_send, pkg_recv.at[1 - c], middle)
    to_middle.start()
    near = remote(
        s.at[near_row, pl.ds(0, MSG), :], halo, near_send.at[0], near_recv.at[0], (near_lon, lat)
    )
    near.start()
    tell(rounds.at[0])

    lax.fori_loop(0, I, own_signs, 0)
    for at in (NC, 128 + NC):
        mats[:, at : at + 32, :] = jnp.zeros((I + 1, 32, J), jnp.bfloat16)
    acc[...] = jnp.zeros(acc.shape, jnp.float32)

    wait_lats(0)

    def column_of(rec):
        square = jnp.transpose(jnp.broadcast_to(rec[0, 8:9, :], (128, 128)))
        return square[32:48, :], square[48:64, :]

    def spread(v, ed):
        for g in range(SK // 8):
            ed[8 * g : 8 * g + 8, :] = v if g == 0 else roll(v, 128 - 16 * g)

    def spread_signs(rec, ed):
        ints = rec[0, 8:9, :].astype(jnp.int32)
        for w in range(2):
            v = signs(ints, 16)
            ed[SK + 16 * w : SK + 16 * w + 16, :] = v if w == 0 else roll(v, 128 - 16)

    for rec, ed in ((recN, edN), (recS, edS)):
        spread(rec[0, 0:8, :], ed)
        spread_signs(rec, ed)

    sea_n, _ = column_of(recN)
    sea_s, north_s = column_of(recS)
    w_n = north_c * sea * shift_north(sea, sea_n)
    w_s = shift_south(w_n, north_s * sea_s * sea[:, :128])
    cf[3] = w_n
    cf[4] = w_s
    cf[0] = sea * (kap + cf[1] + cf[2] + w_n + w_s)

    def halo_north(i, rows):
        return roll(edN[rows, :], 127 - i)

    def halo_south(i, rows):
        return roll(edS[rows, :], lax.rem(128 - i, 128))

    first, last = lane_iota(8) == 0, lane_iota(8) == 127
    total = jnp.zeros((8, 128), jnp.float32)
    wn_far, ws_far = weight(3, far_row), weight(4, far_row)
    for g in range(NC // 8):
        at = pl.ds(8 * g if g < SK // 8 else SG + 8 * g - SK, 8)
        rows = pl.ds(8 * g, 8)
        here = s[far_row, at, :]
        up = wn_far[:, 128:] * (here[:, 128:] - halo_north(far_row, rows))
        down = ws_far[:, :128] * (here[:, :128] - halo_south(far_row, rows))
        v = jnp.where(last, up, jnp.where(first, down, 0.0))
        total = total + (v if g == 0 else roll(v, 2 * g))
    cor[...] = total
    cor_to = remote(cor, in_cor.at[1 - c], cor_send, cor_recv.at[1 - c], middle)
    cor_to.start()

    pl.semaphore_wait(rounds.at[0], len(peers))
    tell(rounds.at[1])

    def stencil(i, here, across, erows):
        f = weight(0, i) * here
        for w, there in across:
            f = f - w * there
        return (
            f
            - weight(3, i) * shift_north(here, halo_north(i, erows))
            - weight(4, i) * shift_south(here, halo_south(i, erows))
        )

    def to_mats(slot, g, t):
        high = t.astype(jnp.bfloat16)
        mats[slot, pl.ds(16 * g, 16), :] = high
        mats[slot, pl.ds(128 + 16 * g, 16), :] = (t - high.astype(jnp.float32)).astype(jnp.bfloat16)

    def add_gram(slot):
        m = mats[slot]
        acc[...] += lax.dot_general(
            m, m, (((1,), (1,)), ((), ())), preferred_element_type=jnp.float32
        )

    def first_row(i, across):
        for g in range(NC // 16):
            f = stencil(i, s[i, rows_at(g), :], across(g), pl.ds(16 * g, 16))
            if g < SK // 16:
                fl[i + 1, pl.ds(16 * g, 16), :] = weight(5, i) * f
            to_mats(i, g, weight(6, i) * f)
        add_gram(i)

    def inner_first(i, carry):
        first_row(
            i,
            lambda g: (
                (weight(1, i), s[i + 1, rows_at(g), :]),
                (weight(2, i), s[i - 1, rows_at(g), :]),
            ),
        )
        return carry

    lax.fori_loop(1, I - 1, inner_first, 0)

    near.wait_recv()
    east_near = jnp.where(c == 1, halo[EX + 3 : EX + 4, :], co_in[0, I - 1 : I, :])
    w_near[...] = (
        east_near * halo[EX + 2 : EX + 3, :] * oc_in[pl.ds(near_row, 1), :].astype(jnp.float32)
    )
    cf[0, pl.ds(near_row, 1), :] += w_near[...] * oc_in[pl.ds(near_row, 1), :].astype(jnp.float32)
    for w in range(2):
        sgn[0, 16 * w : 16 * w + 16, :] = signs(halo[EX + w : EX + w + 1, :].astype(jnp.int32), 16)
    w_beside = weight(1, (I - 2) * (1 - c))

    def across_near(g):
        if g < SK // 16:
            there = halo[16 * g : 16 * g + 16, :]
        else:
            there = sgn[0, 16 * g - SK : 16 * g - SK + 16, :]
        return (w_near[...], there), (w_beside, s[by_near, rows_at(g), :])

    first_row(near_row, across_near)
    near2 = remote(
        fl.at[near_row + 1, pl.ds(0, SK), :], fl.at[c * (I + 1), pl.ds(0, SK), :],
        near_send.at[1], near_recv.at[1], (near_lon, lat),
    )
    near2.start()

    def ret_to(k):
        d = ((lon, lat4), (far_lon, lat4))[k]
        slot = (I, 0)[k]
        return remote(ret, fl.at[pl.ds(slot, 2)], ret_send.at[k], ret_recv, d)

    @pl.when(c == 1)
    def _():
        for k in range(2):
            remote(pkg, in_pk.at[k], pkg_send, pkg_recv.at[k], middle).wait_recv()
            remote(cor, in_cor.at[k], cor_send, cor_recv.at[k], middle).wait_recv()
        co = [[in_pk[k, PK + r : PK + r + 1, :] for r in range(5)] for k in range(2)]
        edge_w = co[0][3] * co[0][2] * co[1][2]
        roots = [jnp.sqrt(co[k][4]) for k in range(2)]
        ends = [lane_iota(8) == 0, lane_iota(8) == 127]
        for k in range(2):
            for w in range(2):
                sgn[k, 16 * w : 16 * w + 16, :] = signs(co[k][w].astype(jnp.int32), 16)
            ret[k, SK:RET, :] = jnp.broadcast_to(edge_w, (8, J))
        for g in range(NC // 16):
            if g < SK // 16:
                us = [in_pk[k, NC + 16 * g : NC + 16 * g + 16, :] for k in range(2)]
            else:
                us = [sgn[k, 16 * g - SK : 16 * g - SK + 16, :] for k in range(2)]
            d = edge_w * (us[0] - us[1])
            for k in range(2):
                fix = []
                for h in (2 * g, 2 * g + 1):
                    v = in_cor[k] if h == 0 else roll(in_cor[k], 128 - 2 * h)
                    fix.append(
                        jnp.concatenate([jnp.where(ends[n], v, 0.0) for n in range(2)], axis=1)
                    )
                f = in_pk[k, 16 * g : 16 * g + 16, :] + jnp.concatenate(fix, axis=0)
                f = f + d if k == 0 else f - d
                if g < SK // 16:
                    ret[k, 16 * g : 16 * g + 16, :] = co[k][4] * f
                to_mats(I - 1 + k, g, roots[k] * f)
        for k in range(2):
            add_gram(I - 1 + k)

    total = (acc[0:NC, 0:128] + acc[0:NC, 128:256]) + (
        acc[128 : 128 + NC, 0:128] + acc[128 : 128 + NC, 128:256]
    )
    for q in range(PLANE):
        pieces[q] = total[PIECE * q : PIECE * q + PIECE, :]
    pl.semaphore_wait(rounds.at[1], len(peers))
    for q, d in plane:
        remote(pieces.at[q], rs.at[rank], ar_send.at[0], ar_recv.at[0], d).start()
    rs[rank] = pieces[rank]

    def wait_all(ref, n, sem):
        pltpu.make_async_copy(ref.at[pl.ds(0, n)], ref.at[pl.ds(0, n)], sem).wait()

    def second_row(i, carry):
        for g in range(SK // 16):
            rows = pl.ds(16 * g, 16)
            across = (
                (weight(1, i), fl[i + 2, rows, :]),
                (weight(2, i), fl[i, rows, :]),
            )
            out[i, rows, :] = stencil(i, fl[i + 1, rows, :], across, rows)
        return carry

    def store_row(i):
        return pltpu.make_async_copy(out.at[i], image.at[:, i, :], store_sem.at[i])

    pack_edges(1, lambda i, rows: fl[i + 1, rows, :], list(range(1, I - 1)) + [near_row])
    start_lats(1)
    wait_lats(1)
    for rec, ed in ((recN, edN), (recS, edS)):
        spread(rec[1, 0:8, :], ed)
    lax.fori_loop(2, I - 2, second_row, 0)
    for i in range(2, I - 2):
        store_row(i).start()

    wait_all(rs, PLANE - 1, ar_recv.at[0])
    zb[z] = jnp.sum(rs[...], axis=0)
    for d in line:
        remote(zb.at[z], zb.at[z], ar_send.at[1], ar_recv.at[1], d).start()

    @pl.when(c == 1)
    def _():
        for k in range(2):
            ret_to(k).start()

    wait_all(zb, NZ - 1, ar_recv.at[1])
    ag[rank] = jnp.sum(zb[...], axis=0) * (1.0 / CELLS)
    for _, d in plane:
        remote(ag.at[rank], ag.at[rank], ar_send.at[2], ar_recv.at[2], d).start()

    near2.wait_recv()
    cf[1, I - 1 : I, :] = jnp.where(c == 1, cf[1, I - 1 : I, :], w_near[...])
    cf[2, 0:1, :] = jnp.where(c == 1, w_near[...], cf[2, 0:1, :])
    second_row(near_row, 0)
    second_row(by_near, 0)
    pl.when(c == 1)(lambda: store_row(0).start())
    pl.when(c == 0)(lambda: store_row(I - 1).start())

    remote(ret, fl.at[pl.ds(I * c, 2)], ret_send.at[0], ret_recv, middle).wait_recv()
    pack_edges(2, lambda i, rows: fl[i + 1, rows, :], [far_row])
    start_lats(2)
    edge_w = fl[(I + 1) * c, SK : SK + 1, :]
    cf[1, I - 1 : I, :] = jnp.where(c == 1, edge_w, w_near[...])
    cf[2, 0:1, :] = jnp.where(c == 1, w_near[...], edge_w)
    cf[0, pl.ds(far_row, 1), :] += edge_w * oc_in[pl.ds(far_row, 1), :].astype(jnp.float32)
    second_row(by_far, 0)
    store_row(1).start()
    store_row(I - 2).start()
    wait_lats(2)
    for rec, ed in ((recN, edN), (recS, edS)):
        spread(rec[1, 0:8, :] + rec[2, 0:8, :], ed)
    second_row(far_row, 0)
    pl.when(c == 1)(lambda: store_row(I - 1).start())
    pl.when(c == 0)(lambda: store_row(0).start())

    wait_all(rs, PLANE - 1, ar_send.at[0])
    wait_all(zb, NZ - 1, ar_send.at[1])
    to_middle.wait_send()
    cor_to.wait_send()
    near.wait_send()
    near2.wait_send()

    @pl.when(c == 1)
    def _():
        for k in range(2):
            ret_to(k).wait_send()

    for i in range(I):
        store_row(i).wait()
    wait_all(ag, PLANE - 1, ar_recv.at[2])
    wait_all(ag, PLANE - 1, ar_send.at[2])
    for q in range(PLANE):
        gram[PIECE * q : PIECE * q + PIECE, :] = ag[q, :, 0:NC]


def finish(image, gram, image_out, gram_out, sems):
    copies = [pltpu.make_async_copy(gram, gram_out, sems.at[4])]
    for k in range(4):
        part = pl.ds(k * (SK // 4), SK // 4)
        copies.append(pltpu.make_async_copy(image.at[part], image_out.at[part], sems.at[k]))
    for copy in copies:
        copy.start()
    for copy in copies:
        copy.wait()


def local(sketch, probe_bits, ocean, east_cond, north_cond, kappa_sq, inv_area):
    f32 = jnp.float32

    def vmem(*shape, kind=f32):
        return pltpu.VMEM(shape, kind)

    dma = pltpu.SemaphoreType.DMA
    any_space = pl.BlockSpec(memory_space=pl.ANY)
    image, gram = pl.pallas_call(
        kernel,
        out_shape=(
            pltpu.VMEM((SK, I, J), f32),
            pltpu.VMEM((NC, NC), f32),
        ),
        in_specs=[pl.BlockSpec(memory_space=pltpu.HBM)] * 7,
        out_specs=(any_space, pl.BlockSpec(memory_space=pltpu.VMEM)),
        scratch_shapes=[
            vmem(I, ROWS, J),
            vmem(2, I, J, kind=jnp.int32),
            vmem(I, J, kind=jnp.int32),
            vmem(4, I, J),
            vmem(7, I, J),
            vmem(1, J),
            vmem(MSG, J),
            vmem(2, NP, J),
            vmem(PKG, J),
            vmem(2, PKG, J),
            vmem(8, 128),
            vmem(2, 8, 128),
            vmem(3, 16, 128),
            vmem(3, 16, 128),
            vmem(3, 16, 128),
            vmem(3, 16, 128),
            vmem(NC, 128),
            vmem(NC, 128),
            vmem(I + 2, RET, J),
            vmem(2, RET, J),
            vmem(I, SK, J),
            vmem(I + 1, 256, J, kind=jnp.bfloat16),
            vmem(256, 256),
            vmem(PLANE, PIECE, 128),
            vmem(PLANE, PIECE, 128),
            vmem(NZ, PIECE, 128),
            vmem(PLANE, PIECE, 128),
            dma((I,)),
            dma((6,)),
            dma,
            dma((2,)),
            dma,
            dma((2,)),
            dma((2,)),
            dma,
            dma((2,)),
            dma((2,)),
            pltpu.SemaphoreType.REGULAR((2,)),
            dma((3, 2)),
            dma((3, 2)),
            dma((3,)),
            dma((3,)),
            dma((I,)),
        ],
        compiler_params=pltpu.CompilerParams(
            collective_id=0, has_side_effects=True, vmem_limit_bytes=24 * 2**20
        ),
        name="nystrom",
    )(*[pltpu.with_memory_space_constraint(a, pltpu.HBM) for a in (sketch, probe_bits, ocean, east_cond, north_cond, kappa_sq, inv_area)])
    return pl.pallas_call(
        finish,
        out_shape=(
            jax.ShapeDtypeStruct((SK, I, J), f32),
            jax.ShapeDtypeStruct((NC, NC), f32),
        ),
        in_specs=[pl.BlockSpec(memory_space=pltpu.VMEM)] * 2,
        out_specs=(any_space, any_space),
        scratch_shapes=[dma((5,))],
        name="finish",
    )(*[pltpu.with_memory_space_constraint(a, pltpu.VMEM) for a in (image, gram)])


def solution(mesh):
    cells = P("lon", "lat")
    columns = P(None, "lon", "lat")
    return jax.shard_map(
        local,
        mesh=mesh,
        in_specs=(columns, columns, cells, cells, cells, cells, cells),
        out_specs=(columns, P()),
        check_vma=False,
    )
```
